32 devices in a mesh: group: 4 (over y, x), sub: 8 (over z, core).
Axes of the slice: x: 2, y: 2, z: 4, core: 2. Of those that a mesh axis runs over, the one named last changes fastest.
Arguments:
- load_cases: bfloat16 [4, 8, 1536, 256], P('group', 'sub'), may hold values from -6 to 6
- inv_schur: bfloat16 [4, 8, 1536, 1536], P('group', 'sub'), may hold values from -0.15625 to 0.15625
- schur_blocks: bfloat16 [4, 8, 1536, 1536], P('group', 'sub'), may hold values from -0.15625 to 0.15625
- coarse_basis: float32 [4, 8, 1536], P('group', 'sub'), may hold values from -0.53033006 to 0.53033006
- coarse_map: int32 [4, 8, 12], P('group', 'sub'), may hold values from 0 to 1023
- multiplicity: int32 [4, 8, 12], P('group', 'sub'), may hold values from 2 to 4
- recv_code: int32 [4, 8, 12], P('group', 'sub'), may hold values from 0 to 23, as said below
- send_blocks: int32 [4, 8, 24], P('group', 'sub'), may hold values from -1 to 11, as said below
- coarse_inv: float32 [4, 1024, 1024], P('group', 'sub'), may hold values from -0.1875 to 0.1875
Outputs:
- multipliers: float32 [4, 8, 1536, 256], P('group', 'sub')
The draws below stay inside these ranges and needn't reach their ends.
Inputs may be any that keep to these rules, and one draw needn't show every extreme that they name: `recv_code`: within one subdomain the blocks read distinct codes; in every subdomain all 4 slots of one direction are read. `send_blocks`: entry d * 4 + j is the block a subdomain sends as slot j of direction d, to the subdomain that reads direction d from it; it is -1 exactly where that subdomain reads nothing from the slot.
All inputs are finite; a program needn't handle non-finite values.
Results may differ from the reference program's by a relative error of at most 0.0085.
Values may be sent and summed in bfloat16 or wider, within the bound.
No kernel may reach another device: no remote copies, remote signals or barrier semaphores. Data moves between devices by JAX's collectives and lax.ppermute only.
A program may use at most 64 MiB of HBM per device.

```python
import jax
import jax.numpy as jnp
from jax import lax

NB = 1536
BLK = 128
NBLK = 12
DIRS = 6
CAP = 4
NC = 1024
CASES = 256
ITERS = 2
NGROUP = 4
NSUBD = 8


SHIFTS = ((1, 1), (1, -1), (1, 2), (1, -2), (0, 1), (0, -1))


def neighbour_tables(key):
    seed_key = jax.random.fold_in(key, 4242)
    full_key, order_key, block_key, remote_key = jax.random.split(seed_key, 4)
    devices_all = NGROUP * NSUBD
    slot_total = DIRS * CAP
    code_ids = jnp.arange(slot_total, dtype=jnp.int32)
    full_dir = jax.random.randint(full_key, (devices_all, 1), 0, DIRS, dtype=jnp.int32)
    priority = jax.random.randint(order_key, (devices_all, slot_total), 0, 1 << 20, dtype=jnp.int32) * slot_total + code_ids[None, :]
    priority = jnp.where(code_ids[None, :] // CAP == full_dir, code_ids[None, :] - slot_total, priority)
    ranking = jnp.argsort(priority, axis=1, stable=True).astype(jnp.int32)
    chosen = ranking[:, :NBLK]
    block_ids = jnp.arange(NBLK, dtype=jnp.int32)
    shuffle_scores = jax.random.randint(block_key, (devices_all, NBLK), 0, 1 << 20, dtype=jnp.int32) * NBLK + block_ids[None, :]
    shuffle = jnp.argsort(shuffle_scores, axis=1, stable=True).astype(jnp.int32)
    recv_flat = jnp.take_along_axis(chosen, shuffle, axis=1)
    used = jnp.sum((chosen[:, :, None] == code_ids[None, None, :]).astype(jnp.int32), axis=1) > 0
    remote = jax.random.randint(remote_key, (devices_all, slot_total), 0, NBLK, dtype=jnp.int32)
    wanted = jnp.where(used, remote, -1).reshape(NGROUP, NSUBD, DIRS, CAP)
    parts = []
    for direction in range(DIRS):
        axis_pos, offset = SHIFTS[direction]
        parts.append(jnp.roll(wanted[:, :, direction], -offset, axis=axis_pos))
    sending = jnp.stack(parts, axis=2).reshape(NGROUP, NSUBD, slot_total)
    return (recv_flat.reshape(NGROUP, NSUBD, NBLK), sending)


def draw_recv_code(key, part):
    return neighbour_tables(key)[0]


def draw_send_blocks(key, part):
    return neighbour_tables(key)[1]


def with_ends(drawn, key, low, largest):
    place = [jax.random.randint(jax.random.fold_in(key, axis), (), 0, length) for axis, length in enumerate(drawn.shape)]
    widest = drawn.shape.index(max(drawn.shape))
    beside = place[:widest] + [(place[widest] + 1) % drawn.shape[widest]] + place[widest + 1:]
    return drawn.at[tuple(place)].set(low).at[tuple(beside)].set(largest)


def steps_of(rng, shape, cuts, low, largest):
    factor_of, own = 1.0, jax.random.fold_in(rng, 6)
    for dim, blocks in cuts:
        draws = jnp.exp(jax.random.uniform(jax.random.fold_in(own, dim), (blocks,), jnp.float32, low / len(cuts), largest / len(cuts)))
        factor_of = factor_of * jnp.repeat(draws, shape[dim] // blocks).reshape([-1 if axis == dim else 1 for axis in range(len(shape))])
    return factor_of


def gaussian(stream_key, extent, deviation, bound, cuts=(), held_as=jnp.bfloat16):
    entries = jax.random.normal(stream_key, extent, jnp.float32) * deviation
    if len(cuts) > 0:
        entries = steps_of(stream_key, extent, cuts, -0.22, 0.18) * entries
    return jnp.clip(entries, min=-bound, max=bound).astype(held_as)


def setup_inputs(seed: int = 0) -> dict:
    splits = jax.random.split(jax.random.key(seed), 10)
    return {
        "load_cases": gaussian(splits[0], (NGROUP, NSUBD, NB, CASES), 1.0, 6.0, ((0, 4), (1, 8))),
        "inv_schur": gaussian(splits[1], (NGROUP, NSUBD, NB, NB), NB ** -0.5, 0.15625, ((0, 4), (1, 8))),
        "schur_blocks": gaussian(splits[2], (NGROUP, NSUBD, NB, NB), NB ** -0.5, 0.15625, ((0, 4), (1, 8))),
        "coarse_basis": gaussian(splits[3], (NGROUP, NSUBD, NB), (2.0 / BLK ** 0.5), 0.53033006, ((0, 4), (1, 8)), jnp.float32),
        "coarse_map": with_ends(jax.random.randint(splits[4], (NGROUP, NSUBD, NBLK), 0, NC), jax.random.fold_in(splits[4], 1), 0, NC - 1).astype(jnp.int32),
        "multiplicity": with_ends(jax.random.randint(splits[5], (NGROUP, NSUBD, NBLK), 2, 5), jax.random.fold_in(splits[5], 1), 2, 4).astype(jnp.int32),
        "recv_code": draw_recv_code(jax.random.fold_in(splits[9], 71), 0),
        "send_blocks": draw_send_blocks(jax.random.fold_in(splits[9], 71), 0),
        "coarse_inv": gaussian(splits[8], (NGROUP, NC, NC), NC ** -0.5, 0.1875, ((0, 4), (1, 8)), jnp.float32),
    }


SHIFTS = ((1, 1), (1, -1), (1, 2), (1, -2), (0, 1), (0, -1))
HIGHEST = lax.Precision.HIGHEST


def jump(values, recv_code, send_blocks):
    pieces = []
    for direction in range(DIRS):
        axis_pos, offset = SHIFTS[direction]
        wanted = send_blocks[:, :, direction * CAP:(direction + 1) * CAP]
        picked = jnp.take_along_axis(values, jnp.maximum(wanted, 0)[:, :, :, None, None], axis=2)
        picked = jnp.where((wanted >= 0)[:, :, :, None, None], picked, jnp.zeros((), jnp.bfloat16))
        pieces.append(jnp.roll(picked, offset, axis=axis_pos))
    received = jnp.concatenate(pieces, axis=2)
    remote = jnp.take_along_axis(received, recv_code[:, :, :, None, None], axis=2)
    return values.astype(jnp.float32) - remote.astype(jnp.float32)


def local_products(matrices, vectors):
    flat_mats = matrices.reshape(NGROUP * NSUBD, NB, NB)
    flat_vecs = vectors.reshape(NGROUP * NSUBD, NB, CASES)
    result = lax.map(lambda pair: jnp.dot(pair[0], pair[1], preferred_element_type=jnp.float32), (flat_mats, flat_vecs))
    return result.reshape(NGROUP, NSUBD, NBLK, BLK, CASES)


def reference(load_cases, inv_schur, schur_blocks, coarse_basis, coarse_map, multiplicity, recv_code, send_blocks, coarse_inv):
    weights = (1.0 / multiplicity.astype(jnp.float32))[:, :, :, None, None]
    basis_rows = coarse_basis.reshape(NGROUP, NSUBD, NBLK, BLK)
    selector = (coarse_map[:, :, :, None] == jnp.arange(NC, dtype=jnp.int32)[None, None, None, :]).astype(jnp.float32)
    multipliers = jnp.zeros((NGROUP, NSUBD, NB, CASES), jnp.float32)
    for iteration in range(ITERS):
        residual_load = (load_cases.astype(jnp.float32) - multipliers).astype(jnp.bfloat16)
        displacement = local_products(inv_schur, residual_load)
        projected = jnp.sum(basis_rows[:, :, :, :, None] * displacement, axis=3)
        coarse_resid = jnp.einsum("gsbk,gsbc->gkc", selector, projected, precision=HIGHEST)
        coarse = jnp.einsum("gjk,gjc->gkc", coarse_inv, coarse_resid, precision=HIGHEST)
        coarse_here = jnp.einsum("gsbk,gkc->gsbc", selector, coarse, precision=HIGHEST)
        corrected = (displacement + basis_rows[:, :, :, :, None] * coarse_here[:, :, :, None, :]).astype(jnp.bfloat16)
        scaled = (jump(corrected, recv_code, send_blocks) * weights).astype(jnp.bfloat16)
        dirichlet = local_products(schur_blocks, scaled)
        dual_step = (dirichlet * weights).astype(jnp.bfloat16)
        multipliers = multipliers + jump(dual_step, recv_code, send_blocks).reshape(NGROUP, NSUBD, NB, CASES)
    return multipliers
```

```python
import functools

import jax
import jax.numpy as jnp
from jax import lax
from jax.experimental import pallas as pl
from jax.experimental.pallas import tpu as pltpu
from jax.sharding import PartitionSpec as P

BLK = 128
DIRS = 6
CAP = 4
ITERS = 2
ROWS = 256
SHIFTS = (("sub", 1), ("sub", -1), ("sub", 2), ("sub", -2), ("group", 1), ("group", -1))
ORDER = (2, 0, 1, 3, 4, 5)
HIGHEST = lax.Precision.HIGHEST
VMEM = pl.BlockSpec(memory_space=pltpu.VMEM)
SMEM = pl.BlockSpec(memory_space=pltpu.SMEM)
ANY = pl.BlockSpec(memory_space=pl.ANY)
PARAMS = pltpu.CompilerParams(vmem_limit_bytes=40 * 1024 * 1024)


def passed_along(block, direction):
    axis, distance = SHIFTS[direction]
    count = lax.axis_size(axis)
    return lax.ppermute(block, axis, [((i - distance) % count, i) for i in range(count)])


def jump_slabs(slabs):
    arrived = {d: passed_along(slabs[d], d) for d in ORDER}
    return [arrived[d] for d in range(DIRS)]


def matrix_copies(matrix, held, sems):
    steps = held.shape[0] // ROWS
    return [
        pltpu.make_async_copy(
            matrix.at[pl.ds(i * ROWS, ROWS)], held.at[pl.ds(i * ROWS, ROWS)], sems.at[i]
        )
        for i in range(steps)
    ]


def slab_copies(slabs, received, sems):
    return [
        pltpu.make_async_copy(slab, received.at[pl.ds(d * CAP, CAP)], sems.at[d])
        for d, slab in enumerate(slabs)
    ]


def pick_blocks(send, values, slabs):
    for d in range(DIRS):
        for j in range(CAP):
            slabs[d][j] = values[send[d * CAP + j]]


def solve_tail(send, held, rhs, copies, basis, disp, proj, slabs, narrow):
    block_count, _, cases = disp.shape
    per = ROWS // BLK
    wide = cases // BLK
    for i, copy in enumerate(copies):
        copy.wait()
        part = jnp.dot(
            held[pl.ds(i * ROWS, ROWS), :], rhs[...], preferred_element_type=jnp.float32
        )
        for k in range(per):
            b = i * per + k
            mine = part[k * BLK : (k + 1) * BLK]
            disp[b] = mine
            narrow[b] = mine.astype(jnp.bfloat16)
            column = basis[b]
            for w in range(wide):
                proj[b, pl.ds(w * BLK, BLK)] = jnp.sum(
                    column * mine[:, w * BLK : (w + 1) * BLK], axis=0
                )
    pick_blocks(send, narrow, slabs)


def first_solve_kernel(send, matrix, load, basis, disp, proj, *rest):
    slabs, (held, narrow, sems) = rest[:DIRS], rest[DIRS:]
    copies = matrix_copies(matrix, held, sems)
    for copy in copies:
        copy.start()
    solve_tail(send, held, load, copies, basis, disp, proj, slabs, narrow)


def next_solve_kernel(send, read, matrix, load, basis, dual, *rest):
    arrived, (mult, disp, proj), rest = rest[:DIRS], rest[DIRS : DIRS + 3], rest[DIRS + 3 :]
    slabs, (held, narrow, received, rhs, sems, slab_sems) = rest[:DIRS], rest[DIRS:]
    incoming = slab_copies(arrived, received, slab_sems)
    copies = matrix_copies(matrix, held, sems)
    for copy in incoming + copies:
        copy.start()
    for copy in incoming:
        copy.wait()
    for b in range(disp.shape[0]):
        step = dual[b].astype(jnp.float32) - received[read[b]].astype(jnp.float32)
        mult[b] = step
        rows = pl.ds(b * BLK, BLK)
        rhs[rows, :] = (load[rows, :].astype(jnp.float32) - step).astype(jnp.bfloat16)
    solve_tail(send, held, rhs, copies, basis, disp, proj, slabs, narrow)


def dirichlet_kernel(
    send, read, weights, matrix, disp, basis, far_basis, coarse, near_rows, up_rows, down_rows, *rest
):
    arrived, dual, rest = rest[:DIRS], rest[DIRS], rest[DIRS + 1 :]
    slabs, (held, received, rows24, rhs, sems, slab_sems) = rest[:DIRS], rest[DIRS:]
    incoming = slab_copies(arrived, received, slab_sems)
    copies = matrix_copies(matrix, held, sems)
    for copy in incoming + copies:
        copy.start()
    near = near_rows.shape[0]
    for k in range(near):
        rows24[k] = near_rows[k : k + 1]
    for j in range(CAP):
        rows24[near + j] = up_rows[j : j + 1]
        rows24[near + CAP + j] = down_rows[j : j + 1]
    for copy in incoming:
        copy.wait()
    block_count, _, cases = disp.shape
    for b in range(block_count):
        code = read[b]
        for w in range(cases // BLK):
            cols = pl.ds(w * BLK, BLK)
            own = disp[b, :, cols] + basis[b] * coarse[pl.ds(b, 1), cols]
            far = received[code, :, cols].astype(jnp.float32) + far_basis[b] * rows24[
                code, :, cols
            ]
            gap = own.astype(jnp.bfloat16).astype(jnp.float32) - far.astype(jnp.bfloat16).astype(
                jnp.float32
            )
            rhs[pl.ds(b * BLK, BLK), cols] = (gap * weights[b]).astype(jnp.bfloat16)
    per = ROWS // BLK
    for i, copy in enumerate(copies):
        copy.wait()
        part = jnp.dot(
            held[pl.ds(i * ROWS, ROWS), :], rhs[...], preferred_element_type=jnp.float32
        )
        for k in range(per):
            b = i * per + k
            dual[b] = (part[k * BLK : (k + 1) * BLK] * weights[b]).astype(jnp.bfloat16)
    pick_blocks(send, dual, slabs)


def finish_kernel(read, mult, dual, *rest):
    arrived, out, received, slab_sems = rest[:DIRS], rest[DIRS], rest[DIRS + 1], rest[DIRS + 2]
    incoming = slab_copies(arrived, received, slab_sems)
    for copy in incoming:
        copy.start()
    for copy in incoming:
        copy.wait()
    for b in range(out.shape[0]):
        gap = dual[b].astype(jnp.float32) - received[read[b]].astype(jnp.float32)
        out[b] = mult[b] + gap


def coarse_kernel(send, table, every, coarse, near_rows, up_rows, down_rows, held):
    block_count = coarse.shape[0]
    near = near_rows.shape[0]
    rows = jnp.dot(
        table[...], every[...], preferred_element_type=jnp.float32, precision=HIGHEST
    )
    coarse[...] = rows[:block_count]
    near_rows[...] = rows[block_count : block_count + near]
    for b in range(block_count):
        held[b] = rows[b : b + 1]
    for j in range(CAP):
        up_rows[pl.ds(j, 1), :] = held[send[near + j]]
        down_rows[pl.ds(j, 1), :] = held[send[near + CAP + j]]


def f32(*shape):
    return jax.ShapeDtypeStruct(shape, jnp.float32)


def bf16(*shape):
    return jax.ShapeDtypeStruct(shape, jnp.bfloat16)


def to_everyone(mine):
    count = lax.axis_size("sub")
    return lax.all_to_all(
        jnp.broadcast_to(mine[None], (count,) + mine.shape), "sub", 0, 0, tiled=True
    )


def on_device(
    load_cases,
    inv_schur,
    schur_blocks,
    coarse_basis,
    coarse_map,
    multiplicity,
    recv_code,
    send_blocks,
    coarse_inv,
):
    dofs = inv_schur.shape[2]
    cases = load_cases.shape[3]
    blocks = dofs // BLK
    near = 4 * CAP
    slots = DIRS * CAP
    subs = lax.axis_size("sub")
    here = lax.axis_index("sub")
    solve_matrix = inv_schur[0, 0]
    dirichlet_matrix = schur_blocks[0, 0]
    load = load_cases[0, 0]
    basis = coarse_basis[0, 0].reshape(blocks, BLK)
    basis_columns = jnp.broadcast_to(basis[:, :, None], (blocks, BLK, BLK))
    read = recv_code[0, 0]
    send = jnp.maximum(send_blocks[0, 0], 0)
    weights = 1.0 / multiplicity[0, 0].astype(jnp.float32)
    steps = dofs // ROWS
    slab_shapes = [bf16(CAP, BLK, cases)] * DIRS
    held = pltpu.VMEM((dofs, dofs), jnp.bfloat16)
    values = pltpu.VMEM((blocks, BLK, cases), jnp.bfloat16)
    received = pltpu.VMEM((slots, BLK, cases), jnp.bfloat16)
    rhs = pltpu.VMEM((dofs, cases), jnp.bfloat16)
    sems = pltpu.SemaphoreType.DMA((steps,))
    slab_sems = pltpu.SemaphoreType.DMA((DIRS,))

    disp, proj, *slabs = pl.pallas_call(
        first_solve_kernel,
        out_shape=[f32(blocks, BLK, cases), f32(blocks, cases)] + slab_shapes,
        in_specs=[SMEM, ANY, VMEM, VMEM],
        out_specs=[VMEM] * (2 + DIRS),
        scratch_shapes=[held, values, sems],
        compiler_params=PARAMS,
    )(send, solve_matrix, load, basis_columns)

    width = -(-(blocks + slots) // BLK) * BLK
    names = jnp.concatenate([coarse_map[0, 0], send]).astype(jnp.float32)
    names = jnp.pad(names, (0, width - blocks - slots)).reshape(-1, BLK)
    told = to_everyone(jnp.concatenate([basis, names])).reshape(subs, -1, BLK)
    every_basis = told[:, :blocks]
    numbers = told[:, blocks:].reshape(subs, -1).astype(jnp.int32)
    every_map = numbers[:, :blocks]
    every_send = numbers[:, blocks : blocks + near]
    chosen = every_send[:, :, None] == jnp.arange(blocks, dtype=jnp.int32)
    slot_dofs = jnp.sum(jnp.where(chosen, every_map[:, None, :], 0), axis=2)

    def to_readers(array):
        parts = array.reshape((subs, 4, CAP) + array.shape[2:])
        moved = [jnp.roll(parts[:, d], SHIFTS[d][1], axis=0) for d in range(4)]
        return jnp.concatenate(moved, axis=1)

    wanted = jnp.concatenate([every_map, to_readers(slot_dofs)], axis=1).reshape(-1)
    orders = jnp.arange(coarse_inv.shape[2], dtype=jnp.int32)
    wanted_hot = (wanted[:, None] == orders).astype(jnp.bfloat16)
    columns = lax.dot_general(
        wanted_hot,
        coarse_inv[0].astype(jnp.bfloat16),
        (((1,), (1,)), ((), ())),
        preferred_element_type=jnp.float32,
    ).astype(jnp.bfloat16)
    columns = lax.all_to_all(columns, "sub", 0, 0, tiled=True)
    columns = columns.reshape(subs, blocks + near, -1).transpose(1, 0, 2).reshape(blocks + near, -1)
    every_hot = (every_map.reshape(-1)[:, None] == orders).astype(jnp.bfloat16)
    table = lax.dot_general(
        columns, every_hot, (((1,), (1,)), ((), ())), preferred_element_type=jnp.float32
    )
    slot_basis = jnp.einsum(
        "skb,sbi->ski", chosen.astype(jnp.float32), every_basis, precision=HIGHEST
    )
    near_basis = lax.dynamic_index_in_dim(to_readers(slot_basis), here, 0, keepdims=False)
    far_hot = (send[near:, None] == jnp.arange(blocks, dtype=jnp.int32)).astype(jnp.float32)
    far_rows = jnp.dot(far_hot, basis, precision=HIGHEST)
    all_rows = jnp.concatenate(
        [near_basis, passed_along(far_rows[:CAP], 4), passed_along(far_rows[CAP:], 5)]
    )
    read_hot = (read[:, None] == jnp.arange(slots, dtype=jnp.int32)).astype(jnp.float32)
    read_basis = jnp.dot(read_hot, all_rows, precision=HIGHEST)
    far_columns = jnp.broadcast_to(read_basis[:, :, None], (blocks, BLK, BLK))

    for iteration in range(ITERS):
        arrived = jump_slabs(slabs)
        every_proj = to_everyone(proj).reshape(-1, cases)
        coarse, near_rows, up_rows, down_rows = pl.pallas_call(
            coarse_kernel,
            out_shape=[f32(blocks, cases), f32(near, cases), f32(CAP, cases), f32(CAP, cases)],
            in_specs=[SMEM, VMEM, VMEM],
            out_specs=[VMEM] * 4,
            scratch_shapes=[pltpu.VMEM((blocks, 1, cases), jnp.float32)],
            compiler_params=PARAMS,
        )(send, table, every_proj)
        up_rows = passed_along(up_rows, 4)
        down_rows = passed_along(down_rows, 5)
        dual, *slabs = pl.pallas_call(
            dirichlet_kernel,
            out_shape=[bf16(blocks, BLK, cases)] + slab_shapes,
            in_specs=[SMEM] * 3 + [ANY] + [VMEM] * 7 + [ANY] * DIRS,
            out_specs=[VMEM] * (1 + DIRS),
            scratch_shapes=[held, received, pltpu.VMEM((slots, 1, cases), jnp.float32), rhs, sems, slab_sems],
            compiler_params=PARAMS,
        )(
            send, read, weights, dirichlet_matrix, disp, basis_columns, far_columns,
            coarse, near_rows, up_rows, down_rows, *arrived,
        )
        arrived = jump_slabs(slabs)
        if iteration + 1 < ITERS:
            mult, disp, proj, *slabs = pl.pallas_call(
                next_solve_kernel,
                out_shape=[f32(blocks, BLK, cases), f32(blocks, BLK, cases), f32(blocks, cases)] + slab_shapes,
                in_specs=[SMEM] * 2 + [ANY] + [VMEM] * 3 + [ANY] * DIRS,
                out_specs=[VMEM] * (3 + DIRS),
                scratch_shapes=[held, values, received, rhs, sems, slab_sems],
                compiler_params=PARAMS,
            )(send, read, solve_matrix, load, basis_columns, dual, *arrived)
    out = pl.pallas_call(
        finish_kernel,
        out_shape=f32(blocks, BLK, cases),
        in_specs=[SMEM] + [VMEM] * 2 + [ANY] * DIRS,
        out_specs=VMEM,
        scratch_shapes=[received, slab_sems],
        compiler_params=PARAMS,
    )(read, mult, dual, *arrived)
    return out.reshape(1, 1, dofs, cases)


def solution(mesh):
    split = P("group", "sub")
    return jax.shard_map(
        on_device, mesh=mesh, in_specs=(split,) * 9, out_specs=split, check_vma=False
    )
```

```python
import jax
import jax.numpy as jnp
from jax import lax
from jax.experimental import pallas as pl
from jax.experimental.pallas import tpu as pltpu
from jax.sharding import PartitionSpec as P

BLK = 128
DIRS = 6
CAP = 4
ITERS = 2
NEAR = 4 * CAP
WIDE = 16
ROWS = 256
EXCHANGES = (("sub", 1), ("sub", 2), ("group", 1))
OFFSETS = (1, -1, 2, -2)
ORDER = (3, 2, 1, 0, 4, 5)
HIGHEST = lax.Precision.HIGHEST
VMEM = pl.BlockSpec(memory_space=pltpu.VMEM)
SMEM = pl.BlockSpec(memory_space=pltpu.SMEM)
HBM = pl.BlockSpec(memory_space=pltpu.HBM)
PARAMS = pltpu.CompilerParams(vmem_limit_bytes=24 * 1024 * 1024)


def f32(*shape):
    return jax.ShapeDtypeStruct(shape, jnp.float32)


def bf16(*shape):
    return jax.ShapeDtypeStruct(shape, jnp.bfloat16)


def is_lower(pair):
    axis, distance = EXCHANGES[pair]
    return (lax.axis_index(axis) // distance) % 2 == 0


def exchanged(slab, way):
    axis, distance = EXCHANGES[way // 2]
    count = lax.axis_size(axis)
    route = []
    for i in range(count):
        upward = (i // distance) % 2 == way % 2
        route.append((i, (i + distance if upward else i - distance) % count))
    return lax.ppermute(slab, axis, route)


def swapped(value, bit):
    count = lax.axis_size("sub")
    return lax.ppermute(value, "sub", [(i, i ^ bit) for i in range(count)])


def bits_of(count):
    return [1 << k for k in range(count.bit_length() - 1)]


def gathered(mine):
    held = mine[None]
    for bit in bits_of(lax.axis_size("sub")):
        held = jnp.concatenate([held, swapped(held, bit)])
    return held


def slot_block(send, way, j):
    direction = jnp.where(is_lower(way // 2), way, way ^ 1)
    return jnp.maximum(send[direction * CAP + j], 0)


def slot_read(read, b):
    code = read[b]
    pair = code // (2 * CAP)
    lower = jnp.where(pair == 0, is_lower(0), jnp.where(pair == 1, is_lower(1), is_lower(2)))
    return jnp.where(lower, code ^ CAP, code)


def pick_blocks(send, values, slabs, ways):
    for slab, way in zip(slabs, ways):
        for j in range(CAP):
            slab[j] = values[slot_block(send, way, j)]


def stack_slabs(arrived, received):
    for way, slab in enumerate(arrived):
        for j in range(CAP):
            received[way * CAP + j] = slab[j]


def solve_rows(matrix, rhs, basis, disp, narrow, proj, i):
    per = ROWS // BLK
    part = jnp.dot(matrix[pl.ds(i * ROWS, ROWS), :], rhs[...], preferred_element_type=jnp.float32)
    for k in range(per):
        b = i * per + k
        mine = part[k * BLK : (k + 1) * BLK]
        disp[b] = mine
        narrow[b] = mine.astype(jnp.bfloat16)
        for w in range(mine.shape[1] // BLK):
            cols = slice(w * BLK, (w + 1) * BLK)
            proj[b : b + 1, cols] = jnp.sum(basis[b] * mine[:, cols], axis=0, keepdims=True)


def clear_rest(proj, blocks):
    proj[blocks:, :] = jnp.zeros((proj.shape[0] - blocks, proj.shape[1]), jnp.float32)


def basis_column(row):
    return jnp.broadcast_to(row, (BLK, BLK)).T


def first_solve_kernel(send, matrix, load, basis, disp, proj, basis_columns, *rest):
    slabs, (held, narrow, sems) = rest[:4], rest[4:]
    blocks = disp.shape[0]
    copies = [
        pltpu.make_async_copy(
            matrix.at[pl.ds(i * ROWS, ROWS)], held.at[pl.ds(i * ROWS, ROWS)], sems.at[i]
        )
        for i in range(held.shape[0] // ROWS)
    ]
    for copy in copies:
        copy.start()
    for b in range(blocks):
        basis_columns[b] = basis_column(basis[b : b + 1, :])
    for i, copy in enumerate(copies):
        copy.wait()
        solve_rows(held, load, basis_columns, disp, narrow, proj, i)
    clear_rest(proj, blocks)
    pick_blocks(send, narrow, slabs, range(4))


def next_solve_kernel(send, read, matrix, load, basis_columns, dual, *rest):
    arrived, (mult, disp, proj), rest = rest[:DIRS], rest[DIRS : DIRS + 3], rest[DIRS + 3 :]
    slabs, (narrow, received, rhs) = rest[:4], rest[4:]
    blocks = disp.shape[0]
    stack_slabs(arrived, received)
    for b in range(blocks):
        far = received[slot_read(read, b)]
        step = dual[b].astype(jnp.float32) - far.astype(jnp.float32)
        mult[b] = step
        rows = pl.ds(b * BLK, BLK)
        rhs[rows, :] = (load[rows, :].astype(jnp.float32) - step).astype(jnp.bfloat16)
    for i in range(blocks * BLK // ROWS):
        solve_rows(matrix, rhs, basis_columns, disp, narrow, proj, i)
    clear_rest(proj, blocks)
    pick_blocks(send, narrow, slabs, range(4))


def coarse_kernel(send, table, every, disp, basis_columns, corrected, near_rows, *rest):
    slabs, (ordered,) = rest[:2], rest[2:]
    here = lax.axis_index("sub")
    for t in range(every.shape[0]):
        ordered[t * WIDE : (t + 1) * WIDE, :] = every[t ^ here]
    rows = jnp.dot(
        table[...], ordered[...], preferred_element_type=jnp.float32, precision=HIGHEST
    )
    near_rows[...] = rows[WIDE:]
    for b in range(disp.shape[0]):
        for w in range(disp.shape[2] // BLK):
            cols = slice(w * BLK, (w + 1) * BLK)
            corrected[b, :, cols] = (
                disp[b, :, cols] + basis_columns[b] * rows[b : b + 1, cols]
            ).astype(jnp.bfloat16)
    pick_blocks(send, corrected, slabs, (4, 5))


def dirichlet_kernel(send, read, weights, matrix, corrected, far_basis, near_rows, *rest):
    arrived, dual, rest = rest[:DIRS], rest[DIRS], rest[DIRS + 1 :]
    slabs, (received, rows, rhs) = rest[:DIRS], rest[DIRS:]
    blocks, _, cases = corrected.shape
    stack_slabs(arrived, received)
    for k in range(NEAR):
        rows[k] = near_rows[k : k + 1, :]
    for k in range(NEAR, DIRS * CAP):
        rows[k] = jnp.zeros((1, cases), jnp.float32)
    for b in range(blocks):
        place, code = slot_read(read, b), read[b]
        for w in range(cases // BLK):
            cols = slice(w * BLK, (w + 1) * BLK)
            far = received[place, :, cols].astype(jnp.float32) + far_basis[b] * rows[code, :, cols]
            far = far.astype(jnp.bfloat16).astype(jnp.float32)
            gap = corrected[b, :, cols].astype(jnp.float32) - far
            rhs[b * BLK : (b + 1) * BLK, cols] = (gap * weights[b]).astype(jnp.bfloat16)
    per = ROWS // BLK
    for i in range(blocks // per):
        part = jnp.dot(
            matrix[pl.ds(i * ROWS, ROWS), :], rhs[...], preferred_element_type=jnp.float32
        )
        for k in range(per):
            b = i * per + k
            dual[b] = (part[k * BLK : (k + 1) * BLK] * weights[b]).astype(jnp.bfloat16)
    pick_blocks(send, dual, slabs, range(DIRS))


def finish_kernel(read, mult, dual, *rest):
    arrived, out, received = rest[:DIRS], rest[DIRS], rest[DIRS + 1]
    stack_slabs(arrived, received)
    for b in range(out.shape[0]):
        far = received[slot_read(read, b)]
        out[b] = mult[b] + (dual[b].astype(jnp.float32) - far.astype(jnp.float32))


def share_kernel(dofs, own_rows, share):
    height, order = own_rows.shape
    width = dofs.shape[1]
    here = lax.axis_index("sub")
    hot = (lax.broadcasted_iota(jnp.int32, (order, width), 0) == dofs[...]).astype(jnp.float32)
    columns = jnp.dot(
        own_rows[...].astype(jnp.bfloat16),
        hot.astype(jnp.bfloat16),
        preferred_element_type=jnp.float32,
    )
    mine = lax.broadcasted_iota(jnp.int32, (height, width), 0) + here * height
    rows = (mine == dofs[...]).astype(jnp.float32)
    share[...] = lax.dot_general(
        columns.astype(jnp.bfloat16),
        rows.astype(jnp.bfloat16),
        (((0,), (0,)), ((), ())),
        preferred_element_type=jnp.float32,
    ).astype(jnp.bfloat16)


def table_kernel(read, every_send, shares, every_basis, table, far_columns, hot):
    here = lax.axis_index("sub")
    subs = lax.axis_size("sub")
    width = shares.shape[1]
    blocks = far_columns.shape[0]
    lanes = lax.broadcasted_iota(jnp.int32, (1, width), 1)
    sources = [lax.rem(here - offset + subs, subs) for offset in OFFSETS]
    for b in range(WIDE):
        hot[b : b + 1, :] = (lanes == here * WIDE + b).astype(jnp.float32)
    for k in range(NEAR):
        source = sources[k // CAP]
        place = source * WIDE + every_send[source * NEAR + k]
        hot[WIDE + k : WIDE + k + 1, :] = (lanes == place).astype(jnp.float32)
    table[...] = jnp.dot(
        hot[...].astype(jnp.bfloat16), shares[...], preferred_element_type=jnp.float32
    )
    for b in range(blocks):
        code = jnp.minimum(read[b], NEAR - 1)
        direction = code // CAP
        source = sources[3]
        for d in range(3):
            source = jnp.where(direction == d, sources[d], source)
        block = every_send[source * NEAR + code]
        far_columns[b] = basis_column(every_basis[(source ^ here) * blocks + block])


def on_device(
    load_cases,
    inv_schur,
    schur_blocks,
    coarse_basis,
    coarse_map,
    multiplicity,
    recv_code,
    send_blocks,
    coarse_inv,
):
    dofs = inv_schur.shape[2]
    cases = load_cases.shape[3]
    blocks = dofs // BLK
    subs = lax.axis_size("sub")
    here = lax.axis_index("sub")
    solve_matrix = inv_schur[0, 0]
    dirichlet_matrix = schur_blocks[0, 0]
    load = load_cases[0, 0]
    basis = coarse_basis[0, 0].reshape(blocks, BLK)
    read = recv_code[0, 0]
    send = send_blocks[0, 0]
    weights = 1.0 / multiplicity[0, 0].astype(jnp.float32)
    whole = f32(blocks, BLK, cases)
    halved = bf16(blocks, BLK, cases)
    slab = bf16(CAP, BLK, cases)
    columns = f32(blocks, BLK, BLK)
    values = pltpu.VMEM(halved.shape, jnp.bfloat16)
    received = pltpu.VMEM((DIRS * CAP, BLK, cases), jnp.bfloat16)
    rhs = pltpu.VMEM((dofs, cases), jnp.bfloat16)

    disp, proj, basis_columns, *slabs = pl.pallas_call(
        first_solve_kernel,
        out_shape=[whole, f32(WIDE, cases), columns] + [slab] * 4,
        in_specs=[SMEM, HBM, VMEM, VMEM],
        out_specs=[VMEM] * 7,
        scratch_shapes=[
            pltpu.VMEM((dofs, dofs), jnp.bfloat16),
            values,
            pltpu.SemaphoreType.DMA((dofs // ROWS,)),
        ],
        compiler_params=PARAMS,
    )(send, solve_matrix, load, basis)

    lanes = -(-subs * WIDE // BLK) * BLK
    names = jnp.stack([jnp.pad(coarse_map[0, 0] + 1, (0, WIDE - blocks)), jnp.maximum(send[:NEAR], 0)])
    names = lax.dynamic_update_slice(
        jnp.zeros((2, lanes), jnp.float32), names.astype(jnp.float32), (0, here * WIDE)
    )
    told = gathered(jnp.concatenate([basis, names.reshape(-1, BLK)]))
    every_basis = told[:, :blocks].reshape(subs * blocks, 1, BLK)
    names = jnp.sum(told[:, blocks:], axis=0).reshape(2, lanes).astype(jnp.int32)
    share = pl.pallas_call(
        share_kernel,
        out_shape=bf16(lanes, lanes),
        in_specs=[VMEM] * 2,
        out_specs=VMEM,
        compiler_params=PARAMS,
    )(names[:1] - 1, coarse_inv[0])
    for bit in bits_of(subs):
        share = share + swapped(share, bit)
    table, far_columns = pl.pallas_call(
        table_kernel,
        out_shape=[f32(WIDE + NEAR, lanes), columns],
        in_specs=[SMEM, SMEM, VMEM, VMEM],
        out_specs=[VMEM] * 2,
        scratch_shapes=[pltpu.VMEM((WIDE + NEAR, lanes), jnp.float32)],
        compiler_params=PARAMS,
    )(read, names[1], share, every_basis)

    for iteration in range(ITERS):
        arrived = {way: exchanged(slabs[way], way) for way in ORDER[:4]}
        corrected, near_rows, *far_slabs = pl.pallas_call(
            coarse_kernel,
            out_shape=[halved, f32(NEAR, cases), slab, slab],
            in_specs=[SMEM] + [VMEM] * 4,
            out_specs=[VMEM] * 4,
            scratch_shapes=[pltpu.VMEM((lanes, cases), jnp.float32)],
            compiler_params=PARAMS,
        )(send, table, gathered(proj), disp, basis_columns)
        for way in ORDER[4:]:
            arrived[way] = exchanged(far_slabs[way - 4], way)
        dual, *slabs = pl.pallas_call(
            dirichlet_kernel,
            out_shape=[halved] + [slab] * DIRS,
            in_specs=[SMEM] * 3 + [VMEM] * (4 + DIRS),
            out_specs=[VMEM] * (1 + DIRS),
            scratch_shapes=[received, pltpu.VMEM((DIRS * CAP, 1, cases), jnp.float32), rhs],
            compiler_params=PARAMS,
        )(
            send, read, weights, dirichlet_matrix, corrected, far_columns, near_rows,
            *[arrived[way] for way in range(DIRS)],
        )
        arrived = {way: exchanged(slabs[way], way) for way in ORDER}
        arrived = [arrived[way] for way in range(DIRS)]
        if iteration + 1 < ITERS:
            mult, disp, proj, *slabs = pl.pallas_call(
                next_solve_kernel,
                out_shape=[whole, whole, f32(WIDE, cases)] + [slab] * 4,
                in_specs=[SMEM] * 2 + [VMEM] * (4 + DIRS),
                out_specs=[VMEM] * 7,
                scratch_shapes=[values, received, rhs],
                compiler_params=PARAMS,
            )(send, read, solve_matrix, load, basis_columns, dual, *arrived)
    out = pl.pallas_call(
        finish_kernel,
        out_shape=whole,
        in_specs=[SMEM] + [VMEM] * (2 + DIRS),
        out_specs=VMEM,
        scratch_shapes=[received],
        compiler_params=PARAMS,
    )(read, mult, dual, *arrived)
    return out.reshape(1, 1, dofs, cases)


def solution(mesh):
    split = P("group", "sub")
    return jax.shard_map(
        on_device, mesh=mesh, in_specs=(split,) * 9, out_specs=split, check_vma=False
    )
```

```python
import functools

import jax
import jax.numpy as jnp
from jax import lax
from jax.experimental import pallas as pl
from jax.experimental.pallas import tpu as pltpu
from jax.sharding import PartitionSpec as P

BLK = 128
DIRS = 6
CAP = 4
NEAR = 4 * CAP
ITERS = 2
ROWS = 512
EXCHANGES = (("sub", 1), ("sub", 2), ("group", 1))
OFFSETS = (1, -1, 2, -2)
ORDER = (3, 2, 1, 0, 4, 5)
HIGHEST = lax.Precision.HIGHEST
VMEM = pl.BlockSpec(memory_space=pltpu.VMEM)
SMEM = pl.BlockSpec(memory_space=pltpu.SMEM)
HBM = pl.BlockSpec(memory_space=pltpu.HBM)
MIB = 1024 * 1024
PARAMS = pltpu.CompilerParams(vmem_limit_bytes=20 * MIB)


def f32(*shape):
    return jax.ShapeDtypeStruct(shape, jnp.float32)


def bf16(*shape):
    return jax.ShapeDtypeStruct(shape, jnp.bfloat16)


def in_hbm(array):
    return pltpu.with_memory_space_constraint(array, pltpu.HBM)


def is_lower(pair):
    axis, distance = EXCHANGES[pair]
    return (lax.axis_index(axis) // distance) % 2 == 0


def exchanged(slab, way):
    axis, distance = EXCHANGES[way // 2]
    count = lax.axis_size(axis)
    route = []
    for i in range(count):
        upward = (i // distance) % 2 == way % 2
        route.append((i, (i + distance if upward else i - distance) % count))
    return lax.ppermute(slab, axis, route)


def swapped(value, mask):
    count = lax.axis_size("sub")
    return lax.ppermute(value, "sub", [(i, i ^ mask) for i in range(count)])


def to_chips(chunks):
    return [chunks[0]] + [swapped(chunk, 2 * p) for p, chunk in enumerate(chunks) if p]


def slot_block(send, way, j):
    direction = jnp.where(is_lower(way // 2), way, way ^ 1)
    return jnp.maximum(send[direction * CAP + j], 0)


def slot_read(read, b):
    code = read[b]
    pair = code // (2 * CAP)
    lower = jnp.where(pair == 0, is_lower(0), jnp.where(pair == 1, is_lower(1), is_lower(2)))
    return jnp.where(lower, code ^ CAP, code)


def pick_blocks(send, values, slabs, ways):
    for slab, way in zip(slabs, ways):
        for j in range(CAP):
            slab[j] = values[slot_block(send, way, j)]


def stack_slabs(arrived, received):
    for way, slab in zip(ORDER, arrived):
        for j in range(CAP):
            received[way * CAP + j] = slab[j]


def as_column(row):
    return jnp.broadcast_to(row, (BLK, BLK)).T


def column_parts(cases):
    return [slice(w * BLK, (w + 1) * BLK) for w in range(cases // BLK)]


def matrix_copies(matrix, held, sems):
    return [
        pltpu.make_async_copy(
            matrix.at[pl.ds(i * ROWS, ROWS)], held.at[pl.ds(i * ROWS, ROWS)], sems.at[i]
        )
        for i in range(held.shape[0] // ROWS)
    ]


def each_rows(copies, matrix, rhs, consume):
    per = ROWS // BLK
    for i in range(matrix.shape[0] // ROWS):
        if copies:
            copies[i].wait()
            if i + 2 < len(copies):
                copies[i + 2].start()
        part = jnp.dot(
            matrix[pl.ds(i * ROWS, ROWS), :], rhs[...], preferred_element_type=jnp.float32
        )
        for k in range(per):
            consume(i * per + k, part[k * BLK : (k + 1) * BLK])


def solve(copies, matrix, rhs, columns, disp, narrow, proj):
    blocks = disp.shape[0]

    def consume(b, mine):
        disp[b] = mine
        narrow[b] = mine.astype(jnp.bfloat16)
        for cols in column_parts(mine.shape[1]):
            proj[b : b + 1, cols] = jnp.sum(columns[b] * mine[:, cols], axis=0, keepdims=True)

    proj[blocks:, :] = jnp.zeros((proj.shape[0] - blocks, proj.shape[1]), jnp.float32)
    each_rows(copies, matrix, rhs, consume)


def tell(wide, coarse_map, send, basis, told):
    subs = lax.axis_size("sub")
    here = lax.axis_index("sub")
    blocks = basis.shape[0]
    tall = (told.shape[0] - NEAR) // 2
    place = lax.broadcasted_iota(jnp.int32, (tall, BLK), 0) * BLK + lax.broadcasted_iota(
        jnp.int32, (tall, BLK), 1
    )
    own = jnp.zeros((tall, BLK), jnp.int32)
    for b in range(blocks):
        own = jnp.where(place == here * wide + b, coarse_map[0, b] + 1, own)
    theirs = jnp.zeros((tall, BLK), jnp.int32)
    for k in range(NEAR):
        block = jnp.maximum(send[0, k], 0)
        reader = lax.rem(here + OFFSETS[k // CAP] + subs, subs)
        theirs = jnp.where(place == reader * wide + k, coarse_map[0, block] + 1, theirs)
        told[k : k + 1, :] = basis[block]
    told[NEAR : NEAR + tall, :] = own.astype(jnp.float32)
    told[NEAR + tall :, :] = theirs.astype(jnp.float32)


def first_solve_kernel(wide, send, coarse_map, matrix, load, basis, disp, proj, columns, told, *rest):
    slabs, rest = rest[:4], rest[4:]
    held, rhs, narrow, send_held, map_held, basis_held, rows, sems, more_sems = rest
    blocks = disp.shape[0]
    copies = matrix_copies(matrix, held, sems)
    pairs = ((send, send_held), (coarse_map, map_held), (basis, basis_held), (load, rhs))
    small = [
        pltpu.make_async_copy(source, target, more_sems.at[i])
        for i, (source, target) in enumerate(pairs)
    ]
    for copy in small + copies[:2]:
        copy.start()
    for copy in small[:3]:
        copy.wait()
    for b in range(blocks):
        row = basis_held[:, b * BLK : (b + 1) * BLK]
        rows[b] = row
        columns[b] = as_column(row)
    tell(wide, map_held, send_held, rows, told)
    small[3].wait()
    solve(copies, held, rhs, columns, disp, narrow, proj)
    pick_blocks(send_held.at[0], narrow, slabs, range(4))


def next_solve_kernel(send, read, matrix, load, columns, dual, *rest):
    arrived, (mult, disp, proj), rest = rest[:DIRS], rest[DIRS : DIRS + 3], rest[DIRS + 3 :]
    slabs, (received, rhs, narrow) = rest[:4], rest[4:]
    stack_slabs(arrived, received)
    for b in range(disp.shape[0]):
        far = received[slot_read(read, b)]
        step = dual[b].astype(jnp.float32) - far.astype(jnp.float32)
        mult[b] = step
        rows = pl.ds(b * BLK, BLK)
        rhs[rows, :] = (load[rows, :].astype(jnp.float32) - step).astype(jnp.bfloat16)
    solve([], matrix, rhs, columns, disp, narrow, proj)
    pick_blocks(send, narrow, slabs, range(4))


def coarse_kernel(wide, send, mine, theirs, part, partner, disp, columns, corrected, near, *rest):
    slabs, (ordered,) = rest[:2], rest[2:]
    here = lax.axis_index("sub")
    chips = mine.shape[0]
    cases = disp.shape[2]
    for p in range(chips):
        for e, values in ((0, mine), (1, theirs)):
            at = ((here ^ (2 * p + e)) * wide) // 8 * 8
            ordered[pl.ds(pl.multiple_of(at, 8), wide), :] = values[p, :wide, :].astype(jnp.float32)
    rows = [0.0, 0.0]
    for q, kind, group, cols in pieces_of(ordered.shape[0], cases):
        span = slice(group * wide, (group + 1) * wide)
        table = part[span, cols].astype(jnp.float32) + partner[span, cols].astype(jnp.float32)
        rows[kind] += jnp.dot(
            table,
            ordered[q * BLK : (q + 1) * BLK, :],
            preferred_element_type=jnp.float32,
            precision=HIGHEST,
        )
    near[...] = rows[1]
    for b in range(disp.shape[0]):
        for cols in column_parts(cases):
            corrected[b, :, cols] = (
                disp[b, :, cols] + columns[b] * rows[0][b : b + 1, cols]
            ).astype(jnp.bfloat16)
    pick_blocks(send, corrected, slabs, (4, 5))


def dirichlet_kernel(streamed, send, read, weights, matrix, corrected, far_columns, near, *rest):
    arrived, dual, rest = rest[:DIRS], rest[DIRS], rest[DIRS + 1 :]
    slabs, (received, rows, rhs, *stream) = rest[:DIRS], rest[DIRS:]
    blocks, _, cases = corrected.shape
    copies = []
    if streamed:
        copies = matrix_copies(matrix, *stream)
        matrix = stream[0]
        for copy in copies[:2]:
            copy.start()
    stack_slabs(arrived, received)
    for k in range(NEAR):
        rows[k] = near[k : k + 1, :]
    for k in range(NEAR, DIRS * CAP):
        rows[k] = jnp.zeros((1, cases), jnp.float32)
    for b in range(blocks):
        place, code = slot_read(read, b), read[b]
        for cols in column_parts(cases):
            far = received[place, :, cols].astype(jnp.float32) + far_columns[b] * rows[code, :, cols]
            far = far.astype(jnp.bfloat16).astype(jnp.float32)
            gap = corrected[b, :, cols].astype(jnp.float32) - far
            rhs[b * BLK : (b + 1) * BLK, cols] = (gap * weights[b]).astype(jnp.bfloat16)

    def consume(b, mine):
        dual[b] = (mine * weights[b]).astype(jnp.bfloat16)

    each_rows(copies, matrix, rhs, consume)
    pick_blocks(send, dual, slabs, range(DIRS))


def finish_kernel(read, mult, dual, *rest):
    arrived, (out, received) = rest[:DIRS], rest[DIRS:]
    stack_slabs(arrived, received)
    for b in range(out.shape[0]):
        far = received[slot_read(read, b)]
        out[b] = mult[b] + (dual[b].astype(jnp.float32) - far.astype(jnp.float32))


def pieces_of(lanes, cases):
    across = cases // BLK
    return [
        (i // 2, i % 2, i // across, slice(i % across * BLK, (i % across + 1) * BLK))
        for i in range(2 * (lanes // BLK))
    ]


def share_kernel(wide, read, own_rows, mine, theirs, proj, far_columns, held, *chunks):
    held, chunks = chunks[-1], (held,) + chunks[:-1]
    high, order = own_rows.shape
    subs, here = lax.axis_size("sub"), lax.axis_index("sub")
    chips = mine.shape[0]
    tall = (mine.shape[1] - NEAR) // 2
    blocks = far_columns.shape[0]
    sums = sum(names[p, NEAR:, :] for p in range(chips) for names in (mine, theirs))
    sums = sums.astype(jnp.int32) - 1

    def lanes_of(first):
        return jnp.concatenate([sums[first + r : first + r + 1] for r in range(tall)], axis=1)

    dofs, lanes = (lanes_of(0), lanes_of(tall)), subs * wide
    local = (lax.broadcasted_iota(jnp.int32, (high, lanes), 0) + here * high == dofs[0][:, :lanes])
    local = local.astype(jnp.float32).astype(jnp.bfloat16)
    source = own_rows[...].astype(jnp.bfloat16)
    for kind in range(2):
        pick = lax.broadcasted_iota(jnp.int32, (order, lanes), 0) == dofs[kind][:, :lanes]
        chosen = jnp.dot(
            source,
            pick.astype(jnp.float32).astype(jnp.bfloat16),
            preferred_element_type=jnp.float32,
        )
        held[kind] = lax.dot_general(
            chosen.astype(jnp.bfloat16),
            local,
            (((0,), (0,)), ((), ())),
            preferred_element_type=jnp.float32,
        )
    groups = (chunks[0].shape[0] // wide - 1) // 2
    for p, chunk in enumerate(chunks):
        chunk[:wide, :] = proj[...].astype(jnp.bfloat16)
        for e in range(2):
            reader = 2 * ((here // 2) ^ p) + e
            at = pl.ds(pl.multiple_of(reader * wide, wide), wide)
            for q, kind, group, cols in pieces_of(lanes, chunk.shape[1]):
                top = (1 + e * groups + group) * wide
                chunk[top : top + wide, cols] = held[
                    kind, at, q * BLK : (q + 1) * BLK
                ].astype(jnp.bfloat16)
    for b in range(blocks):
        code = jnp.minimum(read[b], NEAR - 1)
        direction = code // CAP
        offset = jnp.where(
            direction == 0, OFFSETS[0],
            jnp.where(direction == 1, OFFSETS[1], jnp.where(direction == 2, OFFSETS[2], OFFSETS[3])),
        )
        sender = lax.rem(here - offset + subs, subs) ^ here
        found = jnp.zeros((1, BLK), jnp.float32)
        rows = jnp.where(sender % 2 == 0, mine[sender // 2, :NEAR], theirs[sender // 2, :NEAR])
        line = lax.broadcasted_iota(jnp.int32, (NEAR, BLK), 0)
        found = jnp.sum(jnp.where(line == code, rows, 0.0), axis=0, keepdims=True)
        far_columns[b] = as_column(found)


def merge_kernel(wide, *refs):
    arrived, (outgoing, part) = refs[:-2], refs[-2:]
    chips = len(arrived)
    core = lax.axis_index("sub") % 2
    span = part.shape[0]
    for p, chunk in enumerate(arrived):
        outgoing[p, :wide, :] = chunk[:wide, :]
    tables = [
        sum(chunk[wide + e * span : wide + (e + 1) * span, :].astype(jnp.float32) for chunk in arrived)
        for e in range(2)
    ]
    part[...] = jnp.where(core == 0, tables[0], tables[1]).astype(jnp.bfloat16)
    outgoing[chips, :, :] = jnp.where(core == 0, tables[1], tables[0]).astype(jnp.bfloat16)


def on_device(
    load_cases,
    inv_schur,
    schur_blocks,
    coarse_basis,
    coarse_map,
    multiplicity,
    recv_code,
    send_blocks,
    coarse_inv,
):
    dofs = inv_schur.shape[2]
    cases = load_cases.shape[3]
    blocks = dofs // BLK
    subs = lax.axis_size("sub")
    chips = subs // 2
    wide = NEAR * -(-blocks // NEAR)
    lanes = subs * wide
    tall = 4 * -(-lanes // (4 * BLK))
    groups = -(-2 * (lanes // BLK) // (cases // BLK))
    solve_matrix = inv_schur[0, 0]
    dirichlet_matrix = schur_blocks[0, 0]
    load = load_cases[0, 0]
    read = recv_code[0, 0]
    send = send_blocks[0, 0]
    weights = 1.0 / multiplicity[0, 0].astype(jnp.float32)
    whole = f32(blocks, BLK, cases)
    halved = bf16(blocks, BLK, cases)
    slab = bf16(CAP, BLK, cases)
    block_columns = f32(blocks, BLK, BLK)
    received = pltpu.VMEM((DIRS * CAP, BLK, cases), jnp.bfloat16)
    narrow = pltpu.VMEM((blocks, BLK, cases), jnp.bfloat16)
    rhs = pltpu.VMEM((dofs, cases), jnp.bfloat16)
    steps = pltpu.SemaphoreType.DMA((dofs // ROWS,))
    held = pltpu.VMEM((dofs, dofs), jnp.bfloat16)

    disp, proj, columns, told, *slabs = pl.pallas_call(
        functools.partial(first_solve_kernel, wide),
        out_shape=[whole, f32(wide, cases), block_columns, f32(NEAR + 2 * tall, BLK)] + [slab] * 4,
        in_specs=[HBM] * 5,
        out_specs=[VMEM] * 8,
        scratch_shapes=[
            held,
            rhs,
            narrow,
            pltpu.SMEM((1, DIRS * CAP), jnp.int32),
            pltpu.SMEM((1, blocks), jnp.int32),
            pltpu.VMEM((1, dofs), jnp.float32),
            pltpu.VMEM((blocks, 1, BLK), jnp.float32),
            steps,
            pltpu.SemaphoreType.DMA((4,)),
        ],
        compiler_params=PARAMS,
    )(
        in_hbm(send_blocks[0]), in_hbm(coarse_map[0]), in_hbm(solve_matrix), in_hbm(load),
        in_hbm(coarse_basis[0]),
    )
    mine = jnp.stack(to_chips([told] * chips))
    theirs = swapped(mine, 1)
    far_columns, *chunks = pl.pallas_call(
        functools.partial(share_kernel, wide),
        out_shape=[block_columns] + [bf16((1 + 2 * groups) * wide, cases)] * chips,
        in_specs=[SMEM] + [VMEM] * 4,
        out_specs=[VMEM] * (1 + chips),
        scratch_shapes=[pltpu.VMEM((2, lanes, lanes), jnp.float32)],
        compiler_params=PARAMS,
    )(read, coarse_inv[0], mine, theirs, proj)
    outgoing, part = pl.pallas_call(
        functools.partial(merge_kernel, wide),
        out_shape=[bf16(chips + 1, groups * wide, cases), bf16(groups * wide, cases)],
        in_specs=[VMEM] * chips,
        out_specs=[VMEM] * 2,
        compiler_params=PARAMS,
    )(*to_chips(chunks))
    incoming = swapped(outgoing, 1)
    partner = incoming[chips]

    for iteration in range(ITERS):
        arrived = {way: exchanged(slabs[way], way) for way in range(4)}
        if iteration:
            outgoing = jnp.stack(to_chips([proj.astype(jnp.bfloat16)] * chips))
            incoming = swapped(outgoing, 1)
        corrected, near, *far_slabs = pl.pallas_call(
            functools.partial(coarse_kernel, wide),
            out_shape=[halved, f32(NEAR, cases), slab, slab],
            in_specs=[SMEM] + [VMEM] * 6,
            out_specs=[VMEM] * 4,
            scratch_shapes=[pltpu.VMEM((lanes, cases), jnp.float32)],
            compiler_params=PARAMS,
        )(send, outgoing[:chips], incoming[:chips], part, partner, disp, columns)
        for way in (4, 5):
            arrived[way] = exchanged(far_slabs[way - 4], way)
        streamed = iteration == 0
        dual, *slabs = pl.pallas_call(
            functools.partial(dirichlet_kernel, streamed),
            out_shape=[halved] + [slab] * DIRS,
            in_specs=[SMEM] * 3 + [HBM if streamed else VMEM] + [VMEM] * (3 + DIRS),
            out_specs=[VMEM] * (1 + DIRS),
            scratch_shapes=[received, pltpu.VMEM((DIRS * CAP, 1, cases), jnp.float32), rhs]
            + ([held, steps] if streamed else []),
            compiler_params=PARAMS,
        )(
            send, read, weights, in_hbm(dirichlet_matrix) if streamed else dirichlet_matrix,
            corrected, far_columns, near, *[arrived[way] for way in ORDER],
        )
        arrived = [exchanged(slabs[way], way) for way in ORDER]
        if iteration + 1 < ITERS:
            mult, disp, proj, *slabs = pl.pallas_call(
                next_solve_kernel,
                out_shape=[whole, whole, f32(wide, cases)] + [slab] * 4,
                in_specs=[SMEM] * 2 + [VMEM] * (4 + DIRS),
                out_specs=[VMEM] * 7,
                scratch_shapes=[received, rhs, narrow],
                compiler_params=PARAMS,
            )(send, read, solve_matrix, load, columns, dual, *arrived)
    out = pl.pallas_call(
        finish_kernel,
        out_shape=whole,
        in_specs=[SMEM] + [VMEM] * (2 + DIRS),
        out_specs=VMEM,
        scratch_shapes=[received],
        compiler_params=PARAMS,
    )(read, mult, dual, *arrived)
    return out.reshape(1, 1, dofs, cases)


def solution(mesh):
    split = P("group", "sub")
    return jax.shard_map(
        on_device, mesh=mesh, in_specs=(split,) * 9, out_specs=split, check_vma=False
    )
```

```python
import functools

import jax
import jax.numpy as jnp
from jax import lax
from jax.experimental import pallas as pl
from jax.experimental.pallas import tpu as pltpu
from jax.sharding import PartitionSpec as P

BLK = 128
DIRS = 6
CAP = 4
NEAR = 4 * CAP
ITERS = 2
EARLY = 5
ROWS = 512
SHIFTS = {2: 2, 3: -2}
OFFSETS = (1, -1, 2, -2)
ORDER = (2, 1, 3, 0, 4, 5)
HIGHEST = lax.Precision.HIGHEST
VMEM = pl.BlockSpec(memory_space=pltpu.VMEM)
SMEM = pl.BlockSpec(memory_space=pltpu.SMEM)
HBM = pl.BlockSpec(memory_space=pltpu.HBM)
ANY = pl.BlockSpec(memory_space=pl.ANY)
MIB = 1024 * 1024
PARAMS = pltpu.CompilerParams(vmem_limit_bytes=20 * MIB)


def f32(*shape):
    return jax.ShapeDtypeStruct(shape, jnp.float32)


def bf16(*shape):
    return jax.ShapeDtypeStruct(shape, jnp.bfloat16)


def in_hbm(array):
    return pltpu.with_memory_space_constraint(array, pltpu.HBM)


def is_lower(way):
    return lax.axis_index("sub" if way < 2 else "group") % 2 == 0


def exchanged(slab, way):
    axis = "sub" if way < 4 else "group"
    count = lax.axis_size(axis)
    steps = [SHIFTS.get(way, 1 if i % 2 == way % 2 else -1) for i in range(count)]
    return lax.ppermute(slab, axis, [(i, (i + step) % count) for i, step in enumerate(steps)])


def swapped(value, mask):
    count = lax.axis_size("sub")
    return lax.ppermute(value, "sub", [(i, i ^ mask) for i in range(count)])


def to_chips(chunks):
    return [chunks[0]] + [swapped(chunk, 2 * p) for p, chunk in enumerate(chunks) if p]


def slot_block(send, way, j):
    direction = way if way in SHIFTS else jnp.where(is_lower(way), way, way ^ 1)
    return jnp.maximum(send[direction * CAP + j], 0)


def slot_read(read, b):
    code = read[b]
    way = code // CAP
    swap = jnp.where(way < 2, is_lower(0), (way > 3) & is_lower(4))
    return jnp.where(swap, code ^ CAP, code)


def pick_blocks(send, values, slabs, ways):
    for slab, way in zip(slabs, ways):
        for j in range(CAP):
            slab[j] = values[slot_block(send, way, j)]


def stack_slabs(arrived, received):
    for way, slab in zip(ORDER, arrived):
        for j in range(CAP):
            received[way * CAP + j] = slab[j]


def as_column(row):
    return jnp.broadcast_to(row, (BLK, BLK)).T


def column_parts(cases):
    return [slice(w * BLK, (w + 1) * BLK) for w in range(cases // BLK)]


def matrix_copies(matrix, held, sems):
    return [
        pltpu.make_async_copy(
            matrix.at[pl.ds(i * ROWS, ROWS)], held.at[pl.ds(i * ROWS, ROWS)], sems.at[i]
        )
        for i in range(held.shape[0] // ROWS)
    ]


def each_rows(copies, matrix, rhs, consume):
    per = ROWS // BLK
    for i in range(matrix.shape[0] // ROWS):
        if copies:
            copies[i].wait()
            if i + 2 < len(copies):
                copies[i + 2].start()
        part = jnp.dot(
            matrix[pl.ds(i * ROWS, ROWS), :], rhs[...], preferred_element_type=jnp.float32
        )
        for k in range(per):
            consume(i * per + k, part[k * BLK : (k + 1) * BLK])


def solve(copies, matrix, rhs, columns, disp, narrow, proj):
    blocks = disp.shape[0]

    def consume(b, mine):
        disp[b] = mine
        narrow[b] = mine.astype(jnp.bfloat16)
        for cols in column_parts(mine.shape[1]):
            proj[b : b + 1, cols] = jnp.sum(columns[b] * mine[:, cols], axis=0, keepdims=True)

    proj[blocks:, :] = jnp.zeros((proj.shape[0] - blocks, proj.shape[1]), jnp.float32)
    each_rows(copies, matrix, rhs, consume)


def tell(wide, coarse_map, send, basis, told):
    subs = lax.axis_size("sub")
    here = lax.axis_index("sub")
    blocks = basis.shape[0]
    tall = (told.shape[0] - NEAR) // 2
    place = lax.broadcasted_iota(jnp.int32, (tall, BLK), 0) * BLK + lax.broadcasted_iota(
        jnp.int32, (tall, BLK), 1
    )
    own = jnp.zeros((tall, BLK), jnp.int32)
    for b in range(blocks):
        own = jnp.where(place == here * wide + b, coarse_map[0, b] + 1, own)
    theirs = jnp.zeros((tall, BLK), jnp.int32)
    for k in range(NEAR):
        block = jnp.maximum(send[0, k], 0)
        reader = lax.rem(here + OFFSETS[k // CAP] + subs, subs)
        theirs = jnp.where(place == reader * wide + k, coarse_map[0, block] + 1, theirs)
        told[k : k + 1, :] = basis[block]
    told[NEAR : NEAR + tall, :] = own.astype(jnp.float32)
    told[NEAR + tall :, :] = theirs.astype(jnp.float32)


def first_solve_kernel(wide, send, coarse_map, matrix, load, basis, disp, proj, columns, told, *rest):
    slabs, (held, *rest) = rest[:EARLY], rest[EARLY:]
    rhs, narrow, send_held, map_held, basis_held, rows, sems, more_sems = rest
    blocks = disp.shape[0]
    copies = matrix_copies(matrix, held, sems)
    pairs = ((send, send_held), (coarse_map, map_held), (basis, basis_held), (load, rhs))
    small = [
        pltpu.make_async_copy(source, target, more_sems.at[i])
        for i, (source, target) in enumerate(pairs)
    ]
    for copy in small + copies[:2]:
        copy.start()
    for copy in small[:3]:
        copy.wait()
    for b in range(blocks):
        row = basis_held[:, b * BLK : (b + 1) * BLK]
        rows[b] = row
        columns[b] = as_column(row)
    tell(wide, map_held, send_held, rows, told)
    small[3].wait()
    solve(copies, held, rhs, columns, disp, narrow, proj)
    pick_blocks(send_held.at[0], narrow, slabs, range(EARLY))


def next_solve_kernel(send, read, matrix, load, columns, dual, *rest):
    arrived, (mult, disp, proj), rest = rest[:DIRS], rest[DIRS : DIRS + 3], rest[DIRS + 3 :]
    *slabs, received, rhs, narrow = rest
    stack_slabs(arrived, received)
    for b in range(disp.shape[0]):
        far = received[slot_read(read, b)]
        step = dual[b].astype(jnp.float32) - far.astype(jnp.float32)
        mult[b] = step
        rows = pl.ds(b * BLK, BLK)
        rhs[rows, :] = (load[rows, :].astype(jnp.float32) - step).astype(jnp.bfloat16)
    solve([], matrix, rhs, columns, disp, narrow, proj)
    pick_blocks(send, narrow, slabs, range(len(slabs)))


def coarse_kernel(wide, chips, bring, send, basis, near_basis, disp, columns, *rest):
    parts, tables, rest = rest[:chips], rest[chips : 2 * chips], rest[2 * chips :]
    if bring:
        matrix, *rest, sem = rest
    (corrected, near), slabs, (ordered, held) = rest[:2], rest[2:4], rest[-2:]
    if bring:
        copy = pltpu.make_async_copy(matrix, rest[4], sem)
        copy.start()
    here = lax.axis_index("sub")
    cases = disp.shape[2]
    for p, part in enumerate(parts):
        for e in range(2):
            at = pl.multiple_of((here ^ (2 * p + e)) * wide, wide)
            ordered[pl.ds(at, wide), :] = part[e * wide : (e + 1) * wide, :].astype(jnp.float32)
    total = sum(table[2 * wide :, :].astype(jnp.float32) for table in tables)
    rows = [0.0, 0.0]
    for q, kind, group, cols in pieces_of(ordered.shape[0], cases):
        rows[kind] += jnp.dot(
            total[group * wide : (group + 1) * wide, cols],
            ordered[q * BLK : (q + 1) * BLK, :],
            preferred_element_type=jnp.float32,
            precision=HIGHEST,
        )
    near[:, :cases] = rows[1]
    near[:, cases:] = near_basis[...]
    for b in range(disp.shape[0]):
        held[b, :, :cases] = rows[0][b : b + 1]
        held[b, :, cases:] = basis[:, b * BLK : (b + 1) * BLK]
    for j in range(CAP):
        slabs[0][j : j + 1, :] = held[slot_block(send, 4, j)]
    for b in range(disp.shape[0]):
        for cols in column_parts(cases):
            corrected[b, :, cols] = (
                disp[b, :, cols] + columns[b] * rows[0][b : b + 1, cols]
            ).astype(jnp.bfloat16)
    pick_blocks(send, corrected, slabs[1:], (5,))
    if bring:
        copy.wait()


def dirichlet_kernel(send, read, weights, matrix, corrected, near, far_rows, *rest):
    arrived, dual, rest = rest[:DIRS], rest[DIRS], rest[DIRS + 1 :]
    slabs, (received, rows, rhs) = rest[:DIRS], rest[DIRS:]
    blocks, _, cases = corrected.shape
    stack_slabs(arrived, received)
    for k in range(NEAR):
        rows[k] = near[k : k + 1, :]
    for k in range(NEAR, DIRS * CAP):
        j = k - NEAR
        rows[k] = far_rows[j : j + 1, :] if j < CAP else jnp.zeros_like(rows[k])
    for b in range(blocks):
        place, code = slot_read(read, b), read[b]
        row = jnp.where(code < NEAR, code, place)
        far_column = as_column(rows[row, :, cases:])
        for cols in column_parts(cases):
            far = received[place, :, cols].astype(jnp.float32) + far_column * rows[row, :, cols]
            far = far.astype(jnp.bfloat16).astype(jnp.float32)
            gap = corrected[b, :, cols].astype(jnp.float32) - far
            rhs[b * BLK : (b + 1) * BLK, cols] = (gap * weights[b]).astype(jnp.bfloat16)

    def consume(b, mine):
        dual[b] = (mine * weights[b]).astype(jnp.bfloat16)

    each_rows([], matrix, rhs, consume)
    pick_blocks(send, dual, slabs, range(DIRS))


def finish_kernel(read, mult, dual, *rest):
    arrived, (out, received, ready, sems) = rest[:DIRS], rest[DIRS:]
    stack_slabs(arrived, received)
    copies = []
    for b in range(out.shape[0]):
        far = received[slot_read(read, b)]
        ready[b] = mult[b] + (dual[b].astype(jnp.float32) - far.astype(jnp.float32))
        copies.append(pltpu.make_async_copy(ready.at[b], out.at[b], sems.at[b]))
        copies[b].start()
    for copy in copies:
        copy.wait()


def pieces_of(lanes, cases):
    across = cases // BLK
    return [
        (i // 2, i % 2, i // across, slice(i % across * BLK, (i % across + 1) * BLK))
        for i in range(2 * (lanes // BLK))
    ]


def share_kernel(wide, own_rows, mine, theirs, proj, *rest):
    near_basis, keep, give, held = rest[-4:]
    high, order = own_rows.shape
    subs, here = lax.axis_size("sub"), lax.axis_index("sub")
    chips = mine.shape[0]
    tall = (mine.shape[1] - NEAR) // 2
    sums = sum(names[p, NEAR:, :] for p in range(chips) for names in (mine, theirs))
    sums = sums.astype(jnp.int32) - 1

    def lanes_of(first):
        return jnp.concatenate([sums[first + r : first + r + 1] for r in range(tall)], axis=1)

    dofs, lanes = (lanes_of(0), lanes_of(tall)), subs * wide
    local = (lax.broadcasted_iota(jnp.int32, (high, lanes), 0) + here * high == dofs[0][:, :lanes])
    local = local.astype(jnp.float32).astype(jnp.bfloat16)
    source = own_rows[...].astype(jnp.bfloat16)
    for kind in range(2):
        pick = lax.broadcasted_iota(jnp.int32, (order, lanes), 0) == dofs[kind][:, :lanes]
        chosen = jnp.dot(
            source,
            pick.astype(jnp.float32).astype(jnp.bfloat16),
            preferred_element_type=jnp.float32,
        )
        held[kind] = lax.dot_general(
            chosen.astype(jnp.bfloat16),
            local,
            (((0,), (0,)), ((), ())),
            preferred_element_type=jnp.float32,
        )
    for e, target in enumerate((keep, give)):
        target[chips, : wide, :] = proj[...].astype(jnp.bfloat16)
        for p in range(chips):
            at = pl.ds(pl.multiple_of((here ^ (2 * p + e)) * wide, wide), wide)
            for q, kind, group, cols in pieces_of(lanes, target.shape[2]):
                target[p, group * wide : (group + 1) * wide, cols] = held[
                    kind, at, q * BLK : (q + 1) * BLK
                ].astype(jnp.bfloat16)
    for k in range(NEAR):
        sender = lax.rem(here - OFFSETS[k // CAP] + subs, subs) ^ here
        p, same = sender // 2, sender % 2 == 0
        near_basis[k : k + 1, :] = jnp.where(same, mine[p, k : k + 1], theirs[p, k : k + 1])


def merge_kernel(wide, chips, keep, got, *rest):
    for p, chunk in enumerate(rest[-chips:]):
        chunk[:wide, :] = keep[chips, :wide, :]
        chunk[wide : 2 * wide, :] = got[chips, :wide, :]
        chunk[2 * wide :, :] = keep[p] + got[p]


def on_device(
    load_cases,
    inv_schur,
    schur_blocks,
    coarse_basis,
    coarse_map,
    multiplicity,
    recv_code,
    send_blocks,
    coarse_inv,
):
    dofs = inv_schur.shape[2]
    cases = load_cases.shape[3]
    blocks = dofs // BLK
    subs = lax.axis_size("sub")
    chips = subs // 2
    wide = NEAR * -(-blocks // NEAR)
    lanes = subs * wide
    tall = 4 * -(-lanes // (4 * BLK))
    groups = -(-2 * (lanes // BLK) // (cases // BLK))
    solve_matrix = inv_schur[0, 0]
    dirichlet_matrix = schur_blocks[0, 0]
    load = load_cases[0, 0]
    read = recv_code[0, 0]
    send = send_blocks[0, 0]
    weights = 1.0 / multiplicity[0, 0].astype(jnp.float32)
    whole = f32(blocks, BLK, cases)
    halved = bf16(blocks, BLK, cases)
    slab = bf16(CAP, BLK, cases)
    block_columns = f32(blocks, BLK, BLK)
    received = pltpu.VMEM((DIRS * CAP, BLK, cases), jnp.bfloat16)
    narrow = pltpu.VMEM((blocks, BLK, cases), jnp.bfloat16)
    rhs = pltpu.VMEM((dofs, cases), jnp.bfloat16)
    steps = pltpu.SemaphoreType.DMA((dofs // ROWS,))
    resident = pltpu.VMEM((dofs, dofs), jnp.bfloat16)

    disp, proj, columns, told, *slabs, solve_matrix = pl.pallas_call(
        functools.partial(first_solve_kernel, wide),
        out_shape=[whole, f32(wide, cases), block_columns, f32(NEAR + 2 * tall, BLK)]
        + [slab] * EARLY
        + [resident],
        in_specs=[HBM] * 5,
        out_specs=[VMEM] * (5 + EARLY),
        scratch_shapes=[
            rhs,
            narrow,
            pltpu.SMEM((1, DIRS * CAP), jnp.int32),
            pltpu.SMEM((1, blocks), jnp.int32),
            pltpu.VMEM((1, dofs), jnp.float32),
            pltpu.VMEM((blocks, 1, BLK), jnp.float32),
            steps,
            pltpu.SemaphoreType.DMA((4,)),
        ],
        compiler_params=PARAMS,
    )(
        in_hbm(send_blocks[0]), in_hbm(coarse_map[0]), in_hbm(solve_matrix), in_hbm(load),
        in_hbm(coarse_basis[0]),
    )
    arrived = {way: exchanged(slabs[way], way) for way in ORDER if way < EARLY}
    mine = jnp.stack(to_chips([told] * chips))
    theirs = swapped(mine, 1)
    outgoing = bf16(chips + 1, groups * wide, cases)
    near_basis, keep, give = pl.pallas_call(
        functools.partial(share_kernel, wide),
        out_shape=[f32(NEAR, BLK), outgoing, outgoing],
        in_specs=[VMEM] * 4 + [ANY] * 1,
        out_specs=[VMEM] * 3,
        scratch_shapes=[pltpu.VMEM((2, lanes, lanes), jnp.float32)],
        compiler_params=PARAMS,
    )(coarse_inv[0], mine, theirs, proj, arrived[4])
    chunks = pl.pallas_call(
        functools.partial(merge_kernel, wide, chips),
        out_shape=[bf16((2 + groups) * wide, cases)] * chips,
        in_specs=[VMEM] * 2 + [ANY] * 0,
        out_specs=[VMEM] * chips,
        compiler_params=PARAMS,
    )(keep, swapped(give, 1))
    parts = tables = to_chips(chunks)

    for iteration in range(ITERS):
        bring = iteration == 0
        if iteration:
            arrived = {way: exchanged(slabs[way], way) for way in ORDER if way < EARLY}
            proj = proj.astype(jnp.bfloat16)
            parts = to_chips([jnp.concatenate([proj, swapped(proj, 1)])] * chips)
        corrected, near, *far = pl.pallas_call(
            functools.partial(coarse_kernel, wide, chips, bring),
            out_shape=[halved, f32(NEAR, cases + BLK), f32(CAP, cases + BLK), slab]
            + [resident] * bring,
            in_specs=[SMEM] + [VMEM] * (4 + 2 * chips) + [HBM] * bring,
            out_specs=[VMEM] * (4 + bring),
            scratch_shapes=[
                pltpu.VMEM((lanes, cases), jnp.float32),
                pltpu.VMEM((blocks, 1, cases + BLK), jnp.float32),
            ]
            + [pltpu.SemaphoreType.DMA] * bring,
            compiler_params=PARAMS,
        )(
            send, coarse_basis[0], near_basis, disp, columns, *parts, *tables,
            *[in_hbm(dirichlet_matrix)] * bring,
        )
        if bring:
            *far, dirichlet_matrix = far
        far_rows, arrived[5] = [exchanged(far[way - 4], way) for way in (4, 5)]
        dual, *slabs = pl.pallas_call(
            dirichlet_kernel,
            out_shape=[halved] + [slab] * DIRS,
            in_specs=[SMEM] * 3 + [VMEM] * (4 + DIRS),
            out_specs=[VMEM] * (1 + DIRS),
            scratch_shapes=[received, pltpu.VMEM((DIRS * CAP, 1, cases + BLK), jnp.float32), rhs],
            compiler_params=PARAMS,
        )(
            send, read, weights, dirichlet_matrix, corrected, near, far_rows,
            *[arrived[way] for way in ORDER],
        )
        arrived = [exchanged(slabs[way], way) for way in ORDER]
        if iteration + 1 < ITERS:
            mult, disp, proj, *slabs = pl.pallas_call(
                next_solve_kernel,
                out_shape=[whole, whole, f32(wide, cases)] + [slab] * EARLY,
                in_specs=[SMEM] * 2 + [VMEM] * (4 + DIRS),
                out_specs=[VMEM] * (3 + EARLY),
                scratch_shapes=[received, rhs, narrow],
                compiler_params=PARAMS,
            )(send, read, solve_matrix, load, columns, dual, *arrived)
    out = pl.pallas_call(
        finish_kernel,
        out_shape=whole,
        in_specs=[SMEM] + [VMEM] * (2 + DIRS),
        out_specs=HBM,
        scratch_shapes=[
            received,
            pltpu.VMEM((blocks, BLK, cases), jnp.float32),
            pltpu.SemaphoreType.DMA((blocks,)),
        ],
        compiler_params=PARAMS,
    )(read, mult, dual, *arrived)
    return out.reshape(1, 1, dofs, cases)


def solution(mesh):
    split = P("group", "sub")
    return jax.shard_map(
        on_device, mesh=mesh, in_specs=(split,) * 9, out_specs=split, check_vma=False
    )
```

```python
import functools

import jax
import jax.numpy as jnp
from jax import lax
from jax.experimental import pallas as pl
from jax.experimental.pallas import tpu as pltpu
from jax.sharding import PartitionSpec as P

BLK = 128
DIRS = 6
CAP = 4
NEAR = 4 * CAP
ITERS = 2
EARLY = (5, 5)
ROWS = 512
SHIFTS = {2: 2, 3: -2}
OFFSETS = (1, -1, 2, -2)
ORDER = (2, 1, 3, 0, 4, 5)
HIGHEST = lax.Precision.HIGHEST
VMEM = pl.BlockSpec(memory_space=pltpu.VMEM)
SMEM = pl.BlockSpec(memory_space=pltpu.SMEM)
HBM = pl.BlockSpec(memory_space=pltpu.HBM)
ANY = pl.BlockSpec(memory_space=pl.ANY)
MIB = 1024 * 1024
PARAMS = pltpu.CompilerParams(vmem_limit_bytes=20 * MIB)


def f32(*shape):
    return jax.ShapeDtypeStruct(shape, jnp.float32)


def bf16(*shape):
    return jax.ShapeDtypeStruct(shape, jnp.bfloat16)


def in_hbm(array):
    return pltpu.with_memory_space_constraint(array, pltpu.HBM)


def is_lower(way):
    return lax.axis_index("sub" if way < 2 else "group") % 2 == 0


def exchanged(slab, way):
    axis = "sub" if way < 4 else "group"
    count = lax.axis_size(axis)
    steps = [SHIFTS.get(way, 1 if i % 2 == way % 2 else -1) for i in range(count)]
    return lax.ppermute(slab, axis, [(i, (i + step) % count) for i, step in enumerate(steps)])


def swapped(value, mask):
    count = lax.axis_size("sub")
    return lax.ppermute(value, "sub", [(i, i ^ mask) for i in range(count)])


def to_chips(chunks):
    return [chunks[0]] + [swapped(chunk, 2 * p) for p, chunk in enumerate(chunks) if p]


def slot_block(send, way, j):
    direction = way if way in SHIFTS else jnp.where(is_lower(way), way, way ^ 1)
    return jnp.maximum(send[direction * CAP + j], 0)


def slot_read(read, b):
    code = read[b]
    way = code // CAP
    swap = jnp.where(way < 2, is_lower(0), (way > 3) & is_lower(4))
    return jnp.where(swap, code ^ CAP, code)


def pick_blocks(send, values, slabs, ways):
    for slab, way in zip(slabs, ways):
        for j in range(CAP):
            slab[j] = values[slot_block(send, way, j)]


def stack_slabs(arrived, received):
    for way, slab in zip(ORDER, arrived):
        for j in range(CAP):
            received[way * CAP + j] = slab[j]


def as_column(row):
    return jnp.broadcast_to(row, (BLK, BLK)).T


def column_parts(cases):
    return [slice(w * BLK, (w + 1) * BLK) for w in range(cases // BLK)]


def matrix_copies(matrix, held, sems):
    return [
        pltpu.make_async_copy(
            matrix.at[pl.ds(i * ROWS, ROWS)], held.at[pl.ds(i * ROWS, ROWS)], sems.at[i]
        )
        for i in range(held.shape[0] // ROWS)
    ]


def each_rows(copies, matrix, rhs, consume):
    per = ROWS // BLK
    for i in range(matrix.shape[0] // ROWS):
        if copies:
            copies[i].wait()
            if i + 2 < len(copies):
                copies[i + 2].start()
        part = jnp.dot(
            matrix[pl.ds(i * ROWS, ROWS), :], rhs[...], preferred_element_type=jnp.float32
        )
        for k in range(per):
            consume(i * per + k, part[k * BLK : (k + 1) * BLK])


def solve(copies, matrix, rhs, columns, disp, narrow, proj):
    blocks = disp.shape[0]

    def consume(b, mine):
        disp[b] = mine
        narrow[b] = mine.astype(jnp.bfloat16)
        for cols in column_parts(mine.shape[1]):
            proj[b : b + 1, cols] = jnp.sum(columns[b] * mine[:, cols], axis=0, keepdims=True)

    proj[blocks:, :] = jnp.zeros((proj.shape[0] - blocks, proj.shape[1]), jnp.float32)
    each_rows(copies, matrix, rhs, consume)


def tell(wide, coarse_map, send, basis, told):
    subs = lax.axis_size("sub")
    here = lax.axis_index("sub")
    blocks = basis.shape[0]
    tall = (told.shape[0] - NEAR) // 2
    place = lax.broadcasted_iota(jnp.int32, (tall, BLK), 0) * BLK + lax.broadcasted_iota(
        jnp.int32, (tall, BLK), 1
    )
    own = jnp.zeros((tall, BLK), jnp.int32)
    for b in range(blocks):
        own = jnp.where(place == here * wide + b, coarse_map[0, b] + 1, own)
    theirs = jnp.zeros((tall, BLK), jnp.int32)
    for k in range(NEAR):
        block = jnp.maximum(send[0, k], 0)
        reader = lax.rem(here + OFFSETS[k // CAP] + subs, subs)
        theirs = jnp.where(place == reader * wide + k, coarse_map[0, block] + 1, theirs)
        told[k : k + 1, :] = basis[block]
    told[NEAR : NEAR + tall, :] = own.astype(jnp.float32)
    told[NEAR + tall :, :] = theirs.astype(jnp.float32)


def first_solve_kernel(wide, send, coarse_map, matrix, load, basis, disp, proj, columns, told, *rest):
    slabs, (held, *rest) = rest[: EARLY[0]], rest[EARLY[0] :]
    rhs, narrow, send_held, map_held, basis_held, rows, sems, more_sems = rest
    blocks = disp.shape[0]
    copies = matrix_copies(matrix, held, sems)
    pairs = ((send, send_held), (coarse_map, map_held), (basis, basis_held), (load, rhs))
    small = [
        pltpu.make_async_copy(source, target, more_sems.at[i])
        for i, (source, target) in enumerate(pairs)
    ]
    for copy in small + copies[:2]:
        copy.start()
    for copy in small[:3]:
        copy.wait()
    for b in range(blocks):
        row = basis_held[:, b * BLK : (b + 1) * BLK]
        rows[b] = row
        columns[b] = as_column(row)
    tell(wide, map_held, send_held, rows, told)
    small[3].wait()
    solve(copies, held, rhs, columns, disp, narrow, proj)
    pick_blocks(send_held.at[0], narrow, slabs, range(EARLY[0]))


def next_solve_kernel(send, read, matrix, load, columns, dual, *rest):
    arrived, (mult, disp, proj), rest = rest[:DIRS], rest[DIRS : DIRS + 3], rest[DIRS + 3 :]
    *slabs, received, rhs, narrow = rest
    stack_slabs(arrived, received)
    for b in range(disp.shape[0]):
        far = received[slot_read(read, b)]
        step = dual[b].astype(jnp.float32) - far.astype(jnp.float32)
        mult[b] = step
        rows = pl.ds(b * BLK, BLK)
        rhs[rows, :] = (load[rows, :].astype(jnp.float32) - step).astype(jnp.bfloat16)
    solve([], matrix, rhs, columns, disp, narrow, proj)
    pick_blocks(send, narrow, slabs, range(len(slabs)))


def coarse_kernel(wide, chips, early, bring, ties, send, basis, near_basis, disp, columns, *rest):
    rest = rest[ties:]
    parts, tables, rest = rest[:chips], rest[chips : 2 * chips], rest[2 * chips :]
    if bring:
        matrix, *rest, sem = rest
    (corrected, near), slabs, (ordered, held) = rest[:2], rest[2:4], rest[-2:]
    if bring:
        copy = pltpu.make_async_copy(matrix, rest[4], sem)
        copy.start()
    here = lax.axis_index("sub")
    cases = disp.shape[2]
    for p, part in enumerate(parts):
        for e in range(2):
            at = pl.multiple_of((here ^ (2 * p + e)) * wide, wide)
            ordered[pl.ds(at, wide), :] = part[e * wide : (e + 1) * wide, :].astype(jnp.float32)
    total = sum(table[2 * wide :, :].astype(jnp.float32) for table in tables)
    rows = [0.0, 0.0]
    for q, kind, group, cols in pieces_of(ordered.shape[0], cases):
        rows[kind] += jnp.dot(
            total[group * wide : (group + 1) * wide, cols],
            ordered[q * BLK : (q + 1) * BLK, :],
            preferred_element_type=jnp.float32,
            precision=HIGHEST,
        )
    near[:, :cases] = rows[1]
    near[:, cases:] = near_basis[...]
    if early > 4:
        for b in range(disp.shape[0]):
            held[b, :, :cases] = rows[0][b : b + 1]
            held[b, :, cases:] = basis[:, b * BLK : (b + 1) * BLK]
        for j in range(CAP):
            slabs[0][j : j + 1, :] = held[slot_block(send, 4, j)]
    for b in range(disp.shape[0]):
        for cols in column_parts(cases):
            corrected[b, :, cols] = (
                disp[b, :, cols] + columns[b] * rows[0][b : b + 1, cols]
            ).astype(jnp.bfloat16)
    pick_blocks(send, corrected, slabs[early - 4 :], range(early, DIRS))
    if bring:
        copy.wait()


def dirichlet_kernel(early, send, read, weights, matrix, corrected, near, *rest):
    far_rows, rest = rest[: early - 4], rest[early - 4 :]
    arrived, dual, rest = rest[:DIRS], rest[DIRS], rest[DIRS + 1 :]
    slabs, (received, rows, rhs) = rest[:DIRS], rest[DIRS:]
    blocks, _, cases = corrected.shape
    stack_slabs(arrived, received)
    for k in range(NEAR):
        rows[k] = near[k : k + 1, :]
    for k in range(NEAR, DIRS * CAP):
        j = k - NEAR
        rows[k] = far_rows[0][j : j + 1, :] if far_rows and j < CAP else jnp.zeros_like(rows[k])
    for b in range(blocks):
        place, code = slot_read(read, b), read[b]
        row = jnp.where(code < NEAR, code, place)
        far_column = as_column(rows[row, :, cases:])
        for cols in column_parts(cases):
            far = received[place, :, cols].astype(jnp.float32) + far_column * rows[row, :, cols]
            far = far.astype(jnp.bfloat16).astype(jnp.float32)
            gap = corrected[b, :, cols].astype(jnp.float32) - far
            rhs[b * BLK : (b + 1) * BLK, cols] = (gap * weights[b]).astype(jnp.bfloat16)

    def consume(b, mine):
        dual[b] = (mine * weights[b]).astype(jnp.bfloat16)

    each_rows([], matrix, rhs, consume)
    pick_blocks(send, dual, slabs, range(DIRS))


def finish_kernel(read, mult, dual, *rest):
    arrived, (out, received, ready, sems) = rest[:DIRS], rest[DIRS:]
    stack_slabs(arrived, received)
    copies = []
    for b in range(out.shape[0]):
        far = received[slot_read(read, b)]
        ready[b] = mult[b] + (dual[b].astype(jnp.float32) - far.astype(jnp.float32))
        copies.append(pltpu.make_async_copy(ready.at[b], out.at[b], sems.at[b]))
        copies[b].start()
    for copy in copies:
        copy.wait()


def pieces_of(lanes, cases):
    across = cases // BLK
    return [
        (i // 2, i % 2, i // across, slice(i % across * BLK, (i % across + 1) * BLK))
        for i in range(2 * (lanes // BLK))
    ]


def share_kernel(wide, own_rows, mine, theirs, proj, *rest):
    near_basis, keep, give, held = rest[-4:]
    high, order = own_rows.shape
    subs, here = lax.axis_size("sub"), lax.axis_index("sub")
    chips = mine.shape[0]
    tall = (mine.shape[1] - NEAR) // 2
    sums = sum(names[p, NEAR:, :] for p in range(chips) for names in (mine, theirs))
    sums = sums.astype(jnp.int32) - 1

    def lanes_of(first):
        return jnp.concatenate([sums[first + r : first + r + 1] for r in range(tall)], axis=1)

    dofs, lanes = (lanes_of(0), lanes_of(tall)), subs * wide
    local = (lax.broadcasted_iota(jnp.int32, (high, lanes), 0) + here * high == dofs[0][:, :lanes])
    local = local.astype(jnp.float32).astype(jnp.bfloat16)
    source = own_rows[...].astype(jnp.bfloat16)
    for kind in range(2):
        pick = lax.broadcasted_iota(jnp.int32, (order, lanes), 0) == dofs[kind][:, :lanes]
        chosen = jnp.dot(
            source,
            pick.astype(jnp.float32).astype(jnp.bfloat16),
            preferred_element_type=jnp.float32,
        )
        held[kind] = lax.dot_general(
            chosen.astype(jnp.bfloat16),
            local,
            (((0,), (0,)), ((), ())),
            preferred_element_type=jnp.float32,
        )
    for e, target in enumerate((keep, give)):
        target[chips, : wide, :] = proj[...].astype(jnp.bfloat16)
        for p in range(chips):
            at = pl.ds(pl.multiple_of((here ^ (2 * p + e)) * wide, wide), wide)
            for q, kind, group, cols in pieces_of(lanes, target.shape[2]):
                target[p, group * wide : (group + 1) * wide, cols] = held[
                    kind, at, q * BLK : (q + 1) * BLK
                ].astype(jnp.bfloat16)
    for k in range(NEAR):
        sender = lax.rem(here - OFFSETS[k // CAP] + subs, subs) ^ here
        p, same = sender // 2, sender % 2 == 0
        near_basis[k : k + 1, :] = jnp.where(same, mine[p, k : k + 1], theirs[p, k : k + 1])


def merge_kernel(wide, chips, keep, got, *rest):
    for p, chunk in enumerate(rest[-chips:]):
        chunk[:wide, :] = keep[chips, :wide, :]
        chunk[wide : 2 * wide, :] = got[chips, :wide, :]
        chunk[2 * wide :, :] = keep[p] + got[p]


def on_device(
    load_cases,
    inv_schur,
    schur_blocks,
    coarse_basis,
    coarse_map,
    multiplicity,
    recv_code,
    send_blocks,
    coarse_inv,
):
    dofs = inv_schur.shape[2]
    cases = load_cases.shape[3]
    blocks = dofs // BLK
    subs = lax.axis_size("sub")
    chips = subs // 2
    wide = NEAR * -(-blocks // NEAR)
    lanes = subs * wide
    tall = 4 * -(-lanes // (4 * BLK))
    groups = -(-2 * (lanes // BLK) // (cases // BLK))
    solve_matrix = inv_schur[0, 0]
    dirichlet_matrix = schur_blocks[0, 0]
    load = load_cases[0, 0]
    read = recv_code[0, 0]
    send = send_blocks[0, 0]
    weights = 1.0 / multiplicity[0, 0].astype(jnp.float32)
    whole = f32(blocks, BLK, cases)
    halved = bf16(blocks, BLK, cases)
    slab = bf16(CAP, BLK, cases)
    block_columns = f32(blocks, BLK, BLK)
    received = pltpu.VMEM((DIRS * CAP, BLK, cases), jnp.bfloat16)
    narrow = pltpu.VMEM((blocks, BLK, cases), jnp.bfloat16)
    rhs = pltpu.VMEM((dofs, cases), jnp.bfloat16)
    steps = pltpu.SemaphoreType.DMA((dofs // ROWS,))
    resident = pltpu.VMEM((dofs, dofs), jnp.bfloat16)

    disp, proj, columns, told, *slabs, solve_matrix = pl.pallas_call(
        functools.partial(first_solve_kernel, wide),
        out_shape=[whole, f32(wide, cases), block_columns, f32(NEAR + 2 * tall, BLK)]
        + [slab] * EARLY[0]
        + [resident],
        in_specs=[HBM] * 5,
        out_specs=[VMEM] * (5 + EARLY[0]),
        scratch_shapes=[
            rhs,
            narrow,
            pltpu.SMEM((1, DIRS * CAP), jnp.int32),
            pltpu.SMEM((1, blocks), jnp.int32),
            pltpu.VMEM((1, dofs), jnp.float32),
            pltpu.VMEM((blocks, 1, BLK), jnp.float32),
            steps,
            pltpu.SemaphoreType.DMA((4,)),
        ],
        compiler_params=PARAMS,
    )(
        in_hbm(send_blocks[0]), in_hbm(coarse_map[0]), in_hbm(solve_matrix), in_hbm(load),
        in_hbm(coarse_basis[0]),
    )
    arrived = {way: exchanged(slabs[way], way) for way in ORDER if way < EARLY[0]}
    mine = jnp.stack(to_chips([told] * chips))
    theirs = swapped(mine, 1)
    outgoing = bf16(chips + 1, groups * wide, cases)
    near_basis, keep, give = pl.pallas_call(
        functools.partial(share_kernel, wide),
        out_shape=[f32(NEAR, BLK), outgoing, outgoing],
        in_specs=[VMEM] * 4 + [ANY] * 1,
        out_specs=[VMEM] * 3,
        scratch_shapes=[pltpu.VMEM((2, lanes, lanes), jnp.float32)],
        compiler_params=PARAMS,
    )(coarse_inv[0], mine, theirs, proj, arrived[4])
    chunks = pl.pallas_call(
        functools.partial(merge_kernel, wide, chips),
        out_shape=[bf16((2 + groups) * wide, cases)] * chips,
        in_specs=[VMEM] * 2 + [ANY] * 0,
        out_specs=[VMEM] * chips,
        compiler_params=PARAMS,
    )(keep, swapped(give, 1))
    parts = tables = to_chips(chunks)

    for iteration in range(ITERS):
        bring = iteration == 0
        early = EARLY[iteration]
        if iteration:
            arrived = {way: exchanged(slabs[way], way) for way in ORDER if way < early}
            proj = proj.astype(jnp.bfloat16)
            parts = to_chips([jnp.concatenate([proj, swapped(proj, 1)])] * chips)
        ties = [arrived[way] for way in (() if bring else (4, ))]
        corrected, near, *far = pl.pallas_call(
            functools.partial(coarse_kernel, wide, chips, early, bring, len(ties)),
            out_shape=[halved, f32(NEAR, cases + BLK), f32(CAP, cases + BLK) if early > 4 else slab, slab]
            + [resident] * bring,
            in_specs=[SMEM] + [VMEM] * 4 + [ANY] * len(ties) + [VMEM] * (2 * chips) + [HBM] * bring,
            out_specs=[VMEM] * (4 + bring),
            scratch_shapes=[
                pltpu.VMEM((lanes, cases), jnp.float32),
                pltpu.VMEM((blocks, 1, cases + BLK), jnp.float32),
            ]
            + [pltpu.SemaphoreType.DMA] * bring,
            compiler_params=PARAMS,
        )(
            send, coarse_basis[0], near_basis, disp, columns, *ties, *parts, *tables,
            *[in_hbm(dirichlet_matrix)] * bring,
        )
        if bring:
            *far, dirichlet_matrix = far
        arrived[5] = exchanged(far[1], 5)
        moved = exchanged(far[0], 4)
        if early == 4:
            arrived[4] = moved
        far_rows = [moved] * (early - 4)
        dual, *slabs = pl.pallas_call(
            functools.partial(dirichlet_kernel, early),
            out_shape=[halved] + [slab] * DIRS,
            in_specs=[SMEM] * 3 + [VMEM] * (early - 1 + DIRS),
            out_specs=[VMEM] * (1 + DIRS),
            scratch_shapes=[received, pltpu.VMEM((DIRS * CAP, 1, cases + BLK), jnp.float32), rhs],
            compiler_params=PARAMS,
        )(
            send, read, weights, dirichlet_matrix, corrected, near, *far_rows,
            *[arrived[way] for way in ORDER],
        )
        arrived = [exchanged(slabs[way], way) for way in ORDER]
        if iteration + 1 < ITERS:
            mult, disp, proj, *slabs = pl.pallas_call(
                next_solve_kernel,
                out_shape=[whole, whole, f32(wide, cases)] + [slab] * EARLY[iteration + 1],
                in_specs=[SMEM] * 2 + [VMEM] * (4 + DIRS),
                out_specs=[VMEM] * (3 + EARLY[iteration + 1]),
                scratch_shapes=[received, rhs, narrow],
                compiler_params=PARAMS,
            )(send, read, solve_matrix, load, columns, dual, *arrived)
    out = pl.pallas_call(
        finish_kernel,
        out_shape=whole,
        in_specs=[SMEM] + [VMEM] * (2 + DIRS),
        out_specs=HBM,
        scratch_shapes=[
            received,
            pltpu.VMEM((blocks, BLK, cases), jnp.float32),
            pltpu.SemaphoreType.DMA((blocks,)),
        ],
        compiler_params=PARAMS,
    )(read, mult, dual, *arrived)
    return out.reshape(1, 1, dofs, cases)


def solution(mesh):
    split = P("group", "sub")
    return jax.shard_map(
        on_device, mesh=mesh, in_specs=(split,) * 9, out_specs=split, check_vma=False
    )
```

```python
import functools

import jax
import jax.numpy as jnp
from jax import lax
from jax.experimental import pallas as pl
from jax.experimental.pallas import tpu as pltpu
from jax.sharding import PartitionSpec as P

BLK = 128
DIRS = 6
CAP = 4
NEAR = 4 * CAP
ITERS = 2
EARLY = (5, 5)
ROWS = 512
SHIFTS = {2: 2, 3: -2}
OFFSETS = (1, -1, 2, -2)
ORDER = (2, 1, 3, 0, 4, 5)
HIGHEST = lax.Precision.HIGHEST
VMEM = pl.BlockSpec(memory_space=pltpu.VMEM)
SMEM = pl.BlockSpec(memory_space=pltpu.SMEM)
HBM = pl.BlockSpec(memory_space=pltpu.HBM)
ANY = pl.BlockSpec(memory_space=pl.ANY)
MIB = 1024 * 1024
PARAMS = pltpu.CompilerParams(vmem_limit_bytes=20 * MIB)


def f32(*shape):
    return jax.ShapeDtypeStruct(shape, jnp.float32)


def bf16(*shape):
    return jax.ShapeDtypeStruct(shape, jnp.bfloat16)


def in_hbm(array):
    return pltpu.with_memory_space_constraint(array, pltpu.HBM)


def is_lower(way):
    return lax.axis_index("sub" if way < 2 else "group") % 2 == 0


def exchanged(slab, way):
    axis = "sub" if way < 4 else "group"
    count = lax.axis_size(axis)
    steps = [SHIFTS.get(way, 1 if i % 2 == way % 2 else -1) for i in range(count)]
    return lax.ppermute(slab, axis, [(i, (i + step) % count) for i, step in enumerate(steps)])


def swapped(value, mask):
    count = lax.axis_size("sub")
    return lax.ppermute(value, "sub", [(i, i ^ mask) for i in range(count)])


def to_chips(chunks):
    return [chunks[0]] + [swapped(chunk, 2 * p) for p, chunk in enumerate(chunks) if p]


def slot_block(send, way, j):
    direction = way if way in SHIFTS else jnp.where(is_lower(way), way, way ^ 1)
    return jnp.maximum(send[direction * CAP + j], 0)


def slot_read(read, b):
    code = read[b]
    way = code // CAP
    swap = jnp.where(way < 2, is_lower(0), (way > 3) & is_lower(4))
    return jnp.where(swap, code ^ CAP, code)


def pick_blocks(send, values, slabs, ways):
    for slab, way in zip(slabs, ways):
        for j in range(CAP):
            slab[j] = values[slot_block(send, way, j)]


def stack_slabs(arrived, received):
    for way, slab in zip(ORDER, arrived):
        for j in range(CAP):
            received[way * CAP + j] = slab[j]


def as_column(row):
    return jnp.broadcast_to(row, (BLK, BLK)).T


def column_parts(cases):
    return [slice(w * BLK, (w + 1) * BLK) for w in range(cases // BLK)]


def matrix_copies(matrix, held, sems):
    return [
        pltpu.make_async_copy(
            matrix.at[pl.ds(i * ROWS, ROWS)], held.at[pl.ds(i * ROWS, ROWS)], sems.at[i]
        )
        for i in range(held.shape[0] // ROWS)
    ]


def each_rows(copies, matrix, rhs, consume):
    per = ROWS // BLK
    for i in range(matrix.shape[0] // ROWS):
        if copies:
            copies[i].wait()
            if i + 2 < len(copies):
                copies[i + 2].start()
        part = jnp.dot(
            matrix[pl.ds(i * ROWS, ROWS), :], rhs[...], preferred_element_type=jnp.float32
        )
        for k in range(per):
            consume(i * per + k, part[k * BLK : (k + 1) * BLK])


def solve(copies, matrix, rhs, columns, disp, narrow, proj):
    blocks = disp.shape[0]

    def consume(b, mine):
        disp[b] = mine
        narrow[b] = mine.astype(jnp.bfloat16)
        for cols in column_parts(mine.shape[1]):
            proj[b : b + 1, cols] = jnp.sum(columns[b] * mine[:, cols], axis=0, keepdims=True)

    proj[blocks:, :] = jnp.zeros((proj.shape[0] - blocks, proj.shape[1]), jnp.float32)
    each_rows(copies, matrix, rhs, consume)


def tell(wide, coarse_map, send, basis, told):
    subs = lax.axis_size("sub")
    here = lax.axis_index("sub")
    blocks = basis.shape[0]
    tall = (told.shape[0] - NEAR) // 2
    place = lax.broadcasted_iota(jnp.int32, (tall, BLK), 0) * BLK + lax.broadcasted_iota(
        jnp.int32, (tall, BLK), 1
    )
    own = jnp.zeros((tall, BLK), jnp.int32)
    for b in range(blocks):
        own = jnp.where(place == here * wide + b, coarse_map[0, b] + 1, own)
    theirs = jnp.zeros((tall, BLK), jnp.int32)
    for k in range(NEAR):
        block = jnp.maximum(send[0, k], 0)
        reader = lax.rem(here + OFFSETS[k // CAP] + subs, subs)
        theirs = jnp.where(place == reader * wide + k, coarse_map[0, block] + 1, theirs)
        told[k : k + 1, :] = basis[block]
    told[NEAR : NEAR + tall, :] = own.astype(jnp.float32)
    told[NEAR + tall :, :] = theirs.astype(jnp.float32)


def first_solve_kernel(wide, send, coarse_map, matrix, load, basis, disp, proj, columns, told, *rest):
    slabs, (held, *rest) = rest[: EARLY[0]], rest[EARLY[0] :]
    rhs, narrow, send_held, map_held, basis_held, rows, sems, more_sems = rest
    blocks = disp.shape[0]
    copies = matrix_copies(matrix, held, sems)
    pairs = ((send, send_held), (coarse_map, map_held), (basis, basis_held), (load, rhs))
    small = [
        pltpu.make_async_copy(source, target, more_sems.at[i])
        for i, (source, target) in enumerate(pairs)
    ]
    for copy in small + copies[:2]:
        copy.start()
    for copy in small[:3]:
        copy.wait()
    for b in range(blocks):
        row = basis_held[:, b * BLK : (b + 1) * BLK]
        rows[b] = row
        columns[b] = as_column(row)
    tell(wide, map_held, send_held, rows, told)
    small[3].wait()
    solve(copies, held, rhs, columns, disp, narrow, proj)
    pick_blocks(send_held.at[0], narrow, slabs, range(EARLY[0]))


def next_solve_kernel(send, read, matrix, load, columns, dual, *rest):
    arrived, (mult, disp, proj), rest = rest[:DIRS], rest[DIRS : DIRS + 3], rest[DIRS + 3 :]
    *slabs, received, rhs, narrow = rest
    stack_slabs(arrived, received)
    for b in range(disp.shape[0]):
        far = received[slot_read(read, b)]
        step = dual[b].astype(jnp.float32) - far.astype(jnp.float32)
        mult[b] = step
        rows = pl.ds(b * BLK, BLK)
        rhs[rows, :] = (load[rows, :].astype(jnp.float32) - step).astype(jnp.bfloat16)
    solve([], matrix, rhs, columns, disp, narrow, proj)
    pick_blocks(send, narrow, slabs, range(len(slabs)))


def coarse_kernel(wide, chips, early, ties, send, basis, near_basis, disp, columns, *rest):
    rest = rest[ties:]
    parts, tables, rest = rest[:chips], rest[chips : 2 * chips], rest[2 * chips :]
    corrected, near, *slabs, ordered, held = rest
    here = lax.axis_index("sub")
    cases = disp.shape[2]
    for p, part in enumerate(parts):
        for e in range(2):
            at = pl.multiple_of((here ^ (2 * p + e)) * wide, wide)
            ordered[pl.ds(at, wide), :] = part[e * wide : (e + 1) * wide, :].astype(jnp.float32)
    total = sum(table[2 * wide :, :].astype(jnp.float32) for table in tables)
    rows = [0.0, 0.0]
    for q, kind, group, cols in pieces_of(ordered.shape[0], cases):
        rows[kind] += jnp.dot(
            total[group * wide : (group + 1) * wide, cols],
            ordered[q * BLK : (q + 1) * BLK, :],
            preferred_element_type=jnp.float32,
            precision=HIGHEST,
        )
    near[:, :cases] = rows[1]
    near[:, cases:] = near_basis[...]
    if early > 4:
        for b in range(disp.shape[0]):
            held[b, :, :cases] = rows[0][b : b + 1]
            held[b, :, cases:] = basis[:, b * BLK : (b + 1) * BLK]
        for j in range(CAP):
            slabs[0][j : j + 1, :] = held[slot_block(send, 4, j)]
    for b in range(disp.shape[0]):
        for cols in column_parts(cases):
            corrected[b, :, cols] = (
                disp[b, :, cols] + columns[b] * rows[0][b : b + 1, cols]
            ).astype(jnp.bfloat16)
    pick_blocks(send, corrected, slabs[early - 4 :], range(early, DIRS))


def dirichlet_kernel(early, send, read, weights, matrix, corrected, near, *rest):
    far_rows, rest = rest[: early - 4], rest[early - 4 :]
    arrived, dual, rest = rest[:DIRS], rest[DIRS], rest[DIRS + 1 :]
    slabs, (received, rows, rhs) = rest[:DIRS], rest[DIRS:]
    blocks, _, cases = corrected.shape
    stack_slabs(arrived, received)
    for k in range(NEAR):
        rows[k] = near[k : k + 1, :]
    for k in range(NEAR, DIRS * CAP):
        j = k - NEAR
        rows[k] = far_rows[0][j : j + 1, :] if far_rows and j < CAP else jnp.zeros_like(rows[k])
    for b in range(blocks):
        place, code = slot_read(read, b), read[b]
        row = jnp.where(code < NEAR, code, place)
        far_column = as_column(rows[row, :, cases:])
        for cols in column_parts(cases):
            far = received[place, :, cols].astype(jnp.float32) + far_column * rows[row, :, cols]
            far = far.astype(jnp.bfloat16).astype(jnp.float32)
            gap = corrected[b, :, cols].astype(jnp.float32) - far
            rhs[b * BLK : (b + 1) * BLK, cols] = (gap * weights[b]).astype(jnp.bfloat16)

    def consume(b, mine):
        dual[b] = (mine * weights[b]).astype(jnp.bfloat16)

    each_rows([], matrix, rhs, consume)
    pick_blocks(send, dual, slabs, range(DIRS))


def finish_kernel(read, mult, dual, *rest):
    arrived, (out, received, ready, sems) = rest[:DIRS], rest[DIRS:]
    stack_slabs(arrived, received)
    copies = []
    for b in range(out.shape[0]):
        far = received[slot_read(read, b)]
        ready[b] = mult[b] + (dual[b].astype(jnp.float32) - far.astype(jnp.float32))
        copies.append(pltpu.make_async_copy(ready.at[b], out.at[b], sems.at[b]))
        copies[b].start()
    for copy in copies:
        copy.wait()


def pieces_of(lanes, cases):
    across = cases // BLK
    return [
        (i // 2, i % 2, i // across, slice(i % across * BLK, (i % across + 1) * BLK))
        for i in range(2 * (lanes // BLK))
    ]


def bring_kernel(matrix, after, held, sem):
    copy = pltpu.make_async_copy(matrix, held, sem)
    copy.start()
    copy.wait()


def share_kernel(wide, own_rows, mine, theirs, proj, *rest):
    near_basis, keep, give, held = rest[-4:]
    high, order = own_rows.shape
    subs, here = lax.axis_size("sub"), lax.axis_index("sub")
    chips = mine.shape[0]
    tall = (mine.shape[1] - NEAR) // 2
    sums = sum(names[p, NEAR:, :] for p in range(chips) for names in (mine, theirs))
    sums = sums.astype(jnp.int32) - 1

    def lanes_of(first):
        return jnp.concatenate([sums[first + r : first + r + 1] for r in range(tall)], axis=1)

    dofs, lanes = (lanes_of(0), lanes_of(tall)), subs * wide
    local = (lax.broadcasted_iota(jnp.int32, (high, lanes), 0) + here * high == dofs[0][:, :lanes])
    local = local.astype(jnp.float32).astype(jnp.bfloat16)
    source = own_rows[...].astype(jnp.bfloat16)
    for kind in range(2):
        pick = lax.broadcasted_iota(jnp.int32, (order, lanes), 0) == dofs[kind][:, :lanes]
        chosen = jnp.dot(
            source,
            pick.astype(jnp.float32).astype(jnp.bfloat16),
            preferred_element_type=jnp.float32,
        )
        held[kind] = lax.dot_general(
            chosen.astype(jnp.bfloat16),
            local,
            (((0,), (0,)), ((), ())),
            preferred_element_type=jnp.float32,
        )
    for e, target in enumerate((keep, give)):
        target[chips, : wide, :] = proj[...].astype(jnp.bfloat16)
        for p in range(chips):
            at = pl.ds(pl.multiple_of((here ^ (2 * p + e)) * wide, wide), wide)
            for q, kind, group, cols in pieces_of(lanes, target.shape[2]):
                target[p, group * wide : (group + 1) * wide, cols] = held[
                    kind, at, q * BLK : (q + 1) * BLK
                ].astype(jnp.bfloat16)
    for k in range(NEAR):
        sender = lax.rem(here - OFFSETS[k // CAP] + subs, subs) ^ here
        p, same = sender // 2, sender % 2 == 0
        near_basis[k : k + 1, :] = jnp.where(same, mine[p, k : k + 1], theirs[p, k : k + 1])


def merge_kernel(wide, chips, keep, got, *rest):
    for p, chunk in enumerate(rest[-chips:]):
        chunk[:wide, :] = keep[chips, :wide, :]
        chunk[wide : 2 * wide, :] = got[chips, :wide, :]
        chunk[2 * wide :, :] = keep[p] + got[p]


def on_device(
    load_cases,
    inv_schur,
    schur_blocks,
    coarse_basis,
    coarse_map,
    multiplicity,
    recv_code,
    send_blocks,
    coarse_inv,
):
    dofs = inv_schur.shape[2]
    cases = load_cases.shape[3]
    blocks = dofs // BLK
    subs = lax.axis_size("sub")
    chips = subs // 2
    wide = NEAR * -(-blocks // NEAR)
    lanes = subs * wide
    tall = 4 * -(-lanes // (4 * BLK))
    groups = -(-2 * (lanes // BLK) // (cases // BLK))
    solve_matrix = inv_schur[0, 0]
    dirichlet_matrix = schur_blocks[0, 0]
    load = load_cases[0, 0]
    read = recv_code[0, 0]
    send = send_blocks[0, 0]
    weights = 1.0 / multiplicity[0, 0].astype(jnp.float32)
    whole = f32(blocks, BLK, cases)
    halved = bf16(blocks, BLK, cases)
    slab = bf16(CAP, BLK, cases)
    block_columns = f32(blocks, BLK, BLK)
    received = pltpu.VMEM((DIRS * CAP, BLK, cases), jnp.bfloat16)
    narrow = pltpu.VMEM((blocks, BLK, cases), jnp.bfloat16)
    rhs = pltpu.VMEM((dofs, cases), jnp.bfloat16)
    steps = pltpu.SemaphoreType.DMA((dofs // ROWS,))
    resident = pltpu.VMEM((dofs, dofs), jnp.bfloat16)

    disp, proj, columns, told, *slabs, solve_matrix = pl.pallas_call(
        functools.partial(first_solve_kernel, wide),
        out_shape=[whole, f32(wide, cases), block_columns, f32(NEAR + 2 * tall, BLK)]
        + [slab] * EARLY[0]
        + [resident],
        in_specs=[HBM] * 5,
        out_specs=[VMEM] * (5 + EARLY[0]),
        scratch_shapes=[
            rhs,
            narrow,
            pltpu.SMEM((1, DIRS * CAP), jnp.int32),
            pltpu.SMEM((1, blocks), jnp.int32),
            pltpu.VMEM((1, dofs), jnp.float32),
            pltpu.VMEM((blocks, 1, BLK), jnp.float32),
            steps,
            pltpu.SemaphoreType.DMA((4,)),
        ],
        compiler_params=PARAMS,
    )(
        in_hbm(send_blocks[0]), in_hbm(coarse_map[0]), in_hbm(solve_matrix), in_hbm(load),
        in_hbm(coarse_basis[0]),
    )
    arrived = {way: exchanged(slabs[way], way) for way in ORDER if way < EARLY[0]}
    mine = jnp.stack(to_chips([told] * chips))
    theirs = swapped(mine, 1)
    outgoing = bf16(chips + 1, groups * wide, cases)
    near_basis, keep, give = pl.pallas_call(
        functools.partial(share_kernel, wide),
        out_shape=[f32(NEAR, BLK), outgoing, outgoing],
        in_specs=[VMEM] * 4 + [ANY] * 1,
        out_specs=[VMEM] * 3,
        scratch_shapes=[pltpu.VMEM((2, lanes, lanes), jnp.float32)],
        compiler_params=PARAMS,
    )(coarse_inv[0], mine, theirs, proj, arrived[4])
    chunks = pl.pallas_call(
        functools.partial(merge_kernel, wide, chips),
        out_shape=[bf16((2 + groups) * wide, cases)] * chips,
        in_specs=[VMEM] * 2 + [ANY] * 0,
        out_specs=[VMEM] * chips,
        compiler_params=PARAMS,
    )(keep, swapped(give, 1))
    parts = tables = to_chips(chunks)

    dirichlet_matrix = pl.pallas_call(
        bring_kernel,
        out_shape=resident,
        in_specs=[HBM, ANY],
        out_specs=VMEM,
        scratch_shapes=[pltpu.SemaphoreType.DMA],
        compiler_params=PARAMS,
    )(in_hbm(dirichlet_matrix), proj)

    for iteration in range(ITERS):
        early = EARLY[iteration]
        if iteration:
            arrived = {way: exchanged(slabs[way], way) for way in ORDER if way < early}
            proj = proj.astype(jnp.bfloat16)
            parts = to_chips([jnp.concatenate([proj, swapped(proj, 1)])] * chips)
        ties = [arrived[way] for way in (() if iteration == 0 else (4, 2, ))]
        corrected, near, *far = pl.pallas_call(
            functools.partial(coarse_kernel, wide, chips, early, len(ties)),
            out_shape=[halved, f32(NEAR, cases + BLK), f32(CAP, cases + BLK) if early > 4 else slab, slab],
            in_specs=[SMEM] + [VMEM] * 4 + [ANY] * len(ties) + [VMEM] * (2 * chips),
            out_specs=[VMEM] * 4,
            scratch_shapes=[
                pltpu.VMEM((lanes, cases), jnp.float32),
                pltpu.VMEM((blocks, 1, cases + BLK), jnp.float32),
            ],
            compiler_params=PARAMS,
        )(
            send, coarse_basis[0], near_basis, disp, columns, *ties, *parts, *tables,
        )
        arrived[5] = exchanged(far[1], 5)
        moved = exchanged(far[0], 4)
        if early == 4:
            arrived[4] = moved
        far_rows = [moved] * (early - 4)
        dual, *slabs = pl.pallas_call(
            functools.partial(dirichlet_kernel, early),
            out_shape=[halved] + [slab] * DIRS,
            in_specs=[SMEM] * 3 + [VMEM] * (early - 1 + DIRS),
            out_specs=[VMEM] * (1 + DIRS),
            scratch_shapes=[received, pltpu.VMEM((DIRS * CAP, 1, cases + BLK), jnp.float32), rhs],
            compiler_params=PARAMS,
        )(
            send, read, weights, dirichlet_matrix, corrected, near, *far_rows,
            *[arrived[way] for way in ORDER],
        )
        arrived = [exchanged(slabs[way], way) for way in ORDER]
        if iteration + 1 < ITERS:
            mult, disp, proj, *slabs = pl.pallas_call(
                next_solve_kernel,
                out_shape=[whole, whole, f32(wide, cases)] + [slab] * EARLY[iteration + 1],
                in_specs=[SMEM] * 2 + [VMEM] * (4 + DIRS),
                out_specs=[VMEM] * (3 + EARLY[iteration + 1]),
                scratch_shapes=[received, rhs, narrow],
                compiler_params=PARAMS,
            )(send, read, solve_matrix, load, columns, dual, *arrived)
    out = pl.pallas_call(
        finish_kernel,
        out_shape=whole,
        in_specs=[SMEM] + [VMEM] * (2 + DIRS),
        out_specs=HBM,
        scratch_shapes=[
            received,
            pltpu.VMEM((blocks, BLK, cases), jnp.float32),
            pltpu.SemaphoreType.DMA((blocks,)),
        ],
        compiler_params=PARAMS,
    )(read, mult, dual, *arrived)
    return out.reshape(1, 1, dofs, cases)


def solution(mesh):
    split = P("group", "sub")
    return jax.shard_map(
        on_device, mesh=mesh, in_specs=(split,) * 9, out_specs=split, check_vma=False
    )
```

```python
import functools

import jax
import jax.numpy as jnp
from jax import lax
from jax.experimental import pallas as pl
from jax.experimental.pallas import tpu as pltpu
from jax.sharding import PartitionSpec as P

BLK = 128
DIRS = 6
CAP = 4
NEAR = 4 * CAP
ITERS = 2
EARLY = (5, 5)
ROWS = 512
SHIFTS = {2: 2, 3: -2}
OFFSETS = (1, -1, 2, -2)
ORDER = (2, 1, 3, 0, 4, 5)
SECOND = (2, 1, 3, 4, 5, 0)
HIGHEST = lax.Precision.HIGHEST
VMEM = pl.BlockSpec(memory_space=pltpu.VMEM)
SMEM = pl.BlockSpec(memory_space=pltpu.SMEM)
HBM = pl.BlockSpec(memory_space=pltpu.HBM)
ANY = pl.BlockSpec(memory_space=pl.ANY)
MIB = 1024 * 1024
PARAMS = pltpu.CompilerParams(vmem_limit_bytes=20 * MIB)


def f32(*shape):
    return jax.ShapeDtypeStruct(shape, jnp.float32)


def bf16(*shape):
    return jax.ShapeDtypeStruct(shape, jnp.bfloat16)


def in_hbm(array):
    return pltpu.with_memory_space_constraint(array, pltpu.HBM)


def is_lower(way):
    return lax.axis_index("sub" if way < 2 else "group") % 2 == 0


def exchanged(slab, way):
    axis = "sub" if way < 4 else "group"
    count = lax.axis_size(axis)
    steps = [SHIFTS.get(way, 1 if i % 2 == way % 2 else -1) for i in range(count)]
    return lax.ppermute(slab, axis, [(i, (i + step) % count) for i, step in enumerate(steps)])


def swapped(value, mask):
    count = lax.axis_size("sub")
    return lax.ppermute(value, "sub", [(i, i ^ mask) for i in range(count)])


def to_chips(chunks):
    return [chunks[0]] + [swapped(chunk, 2 * p) for p, chunk in enumerate(chunks) if p]


def slot_block(send, way, j):
    direction = way if way in SHIFTS else jnp.where(is_lower(way), way, way ^ 1)
    return jnp.maximum(send[direction * CAP + j], 0)


def slot_read(read, b):
    code = read[b]
    way = code // CAP
    swap = jnp.where(way < 2, is_lower(0), (way > 3) & is_lower(4))
    return jnp.where(swap, code ^ CAP, code)


def pick_blocks(send, values, slabs, ways):
    for slab, way in zip(slabs, ways):
        for j in range(CAP):
            slab[j] = values[slot_block(send, way, j)]


def stack_slabs(arrived, received, order):
    for way, slab in zip(order, arrived):
        for j in range(CAP):
            received[way * CAP + j] = slab[j]


def as_column(row):
    return jnp.broadcast_to(row, (BLK, BLK)).T


def column_parts(cases):
    return [slice(w * BLK, (w + 1) * BLK) for w in range(cases // BLK)]


def matrix_copies(matrix, held, sems):
    return [
        pltpu.make_async_copy(
            matrix.at[pl.ds(i * ROWS, ROWS)], held.at[pl.ds(i * ROWS, ROWS)], sems.at[i]
        )
        for i in range(held.shape[0] // ROWS)
    ]


def each_rows(copies, matrix, rhs, consume):
    per = ROWS // BLK
    for i in range(matrix.shape[0] // ROWS):
        if copies:
            copies[i].wait()
            if i + 2 < len(copies):
                copies[i + 2].start()
        part = jnp.dot(
            matrix[pl.ds(i * ROWS, ROWS), :], rhs[...], preferred_element_type=jnp.float32
        )
        for k in range(per):
            consume(i * per + k, part[k * BLK : (k + 1) * BLK])


def solve(copies, matrix, rhs, columns, disp, narrow, proj):
    blocks = disp.shape[0]

    def consume(b, mine):
        disp[b] = mine
        narrow[b] = mine.astype(jnp.bfloat16)
        for cols in column_parts(mine.shape[1]):
            proj[b : b + 1, cols] = jnp.sum(columns[b] * mine[:, cols], axis=0, keepdims=True)

    proj[blocks:, :] = jnp.zeros((proj.shape[0] - blocks, proj.shape[1]), jnp.float32)
    each_rows(copies, matrix, rhs, consume)


def tell(wide, coarse_map, send, basis, told):
    subs = lax.axis_size("sub")
    here = lax.axis_index("sub")
    blocks = basis.shape[0]
    tall = (told.shape[0] - NEAR) // 2
    place = lax.broadcasted_iota(jnp.int32, (tall, BLK), 0) * BLK + lax.broadcasted_iota(
        jnp.int32, (tall, BLK), 1
    )
    own = jnp.zeros((tall, BLK), jnp.int32)
    for b in range(blocks):
        own = jnp.where(place == here * wide + b, coarse_map[0, b] + 1, own)
    theirs = jnp.zeros((tall, BLK), jnp.int32)
    for k in range(NEAR):
        block = jnp.maximum(send[0, k], 0)
        reader = lax.rem(here + OFFSETS[k // CAP] + subs, subs)
        theirs = jnp.where(place == reader * wide + k, coarse_map[0, block] + 1, theirs)
        told[k : k + 1, :] = basis[block]
    told[NEAR : NEAR + tall, :] = own.astype(jnp.float32)
    told[NEAR + tall :, :] = theirs.astype(jnp.float32)


def first_solve_kernel(wide, send, coarse_map, matrix, load, basis, disp, proj, columns, told, *rest):
    slabs, (held, *rest) = rest[: EARLY[0]], rest[EARLY[0] :]
    rhs, narrow, send_held, map_held, basis_held, rows, sems, more_sems = rest
    blocks = disp.shape[0]
    copies = matrix_copies(matrix, held, sems)
    pairs = ((send, send_held), (coarse_map, map_held), (basis, basis_held), (load, rhs))
    small = [
        pltpu.make_async_copy(source, target, more_sems.at[i])
        for i, (source, target) in enumerate(pairs)
    ]
    for copy in small + copies[:2]:
        copy.start()
    for copy in small[:3]:
        copy.wait()
    for b in range(blocks):
        row = basis_held[:, b * BLK : (b + 1) * BLK]
        rows[b] = row
        columns[b] = as_column(row)
    small[3].wait()
    solve(copies, held, rhs, columns, disp, narrow, proj)
    tell(wide, map_held, send_held, rows, told)
    pick_blocks(send_held.at[0], narrow, slabs, range(EARLY[0]))


def next_solve_kernel(send, read, matrix, load, columns, dual, *rest):
    arrived, (mult, disp, proj), rest = rest[:DIRS], rest[DIRS : DIRS + 3], rest[DIRS + 3 :]
    *slabs, received, rhs, narrow = rest
    stack_slabs(arrived, received, SECOND)
    for b in range(disp.shape[0]):
        far = received[slot_read(read, b)]
        step = dual[b].astype(jnp.float32) - far.astype(jnp.float32)
        mult[b] = step
        rows = pl.ds(b * BLK, BLK)
        rhs[rows, :] = (load[rows, :].astype(jnp.float32) - step).astype(jnp.bfloat16)
    solve([], matrix, rhs, columns, disp, narrow, proj)
    pick_blocks(send, narrow, slabs, range(len(slabs)))


def coarse_kernel(wide, chips, early, ties, send, basis, near_basis, disp, columns, *rest):
    rest = rest[ties:]
    parts, tables, rest = rest[:chips], rest[chips : 2 * chips], rest[2 * chips :]
    corrected, near, *slabs, ordered, held = rest
    here = lax.axis_index("sub")
    cases = disp.shape[2]
    for p, part in enumerate(parts):
        for e in range(2):
            at = pl.multiple_of((here ^ (2 * p + e)) * wide, wide)
            ordered[pl.ds(at, wide), :] = part[e * wide : (e + 1) * wide, :].astype(jnp.float32)
    total = sum(table[2 * wide :, :].astype(jnp.float32) for table in tables)
    rows = [0.0, 0.0]
    for q, kind, group, cols in pieces_of(ordered.shape[0], cases):
        rows[kind] += jnp.dot(
            total[group * wide : (group + 1) * wide, cols],
            ordered[q * BLK : (q + 1) * BLK, :],
            preferred_element_type=jnp.float32,
            precision=HIGHEST,
        )
    near[:, :cases] = rows[1]
    near[:, cases:] = near_basis[...]
    if early > 4:
        for b in range(disp.shape[0]):
            held[b, :, :cases] = rows[0][b : b + 1]
            held[b, :, cases:] = basis[:, b * BLK : (b + 1) * BLK]
        for j in range(CAP):
            slabs[0][j : j + 1, :] = held[slot_block(send, 4, j)]
    for b in range(disp.shape[0]):
        for cols in column_parts(cases):
            corrected[b, :, cols] = (
                disp[b, :, cols] + columns[b] * rows[0][b : b + 1, cols]
            ).astype(jnp.bfloat16)
    pick_blocks(send, corrected, slabs[early - 4 :], range(early, DIRS))


def dirichlet_kernel(early, send, read, weights, matrix, corrected, near, *rest):
    far_rows, rest = rest[: early - 4], rest[early - 4 :]
    arrived, dual, rest = rest[:DIRS], rest[DIRS], rest[DIRS + 1 :]
    slabs, (received, rows, rhs) = rest[:DIRS], rest[DIRS:]
    blocks, _, cases = corrected.shape
    stack_slabs(arrived, received, ORDER)
    for k in range(NEAR):
        rows[k] = near[k : k + 1, :]
    for k in range(NEAR, DIRS * CAP):
        j = k - NEAR
        rows[k] = far_rows[0][j : j + 1, :] if far_rows and j < CAP else jnp.zeros_like(rows[k])
    for b in range(blocks):
        place, code = slot_read(read, b), read[b]
        row = jnp.where(code < NEAR, code, place)
        far_column = as_column(rows[row, :, cases:])
        for cols in column_parts(cases):
            far = received[place, :, cols].astype(jnp.float32) + far_column * rows[row, :, cols]
            far = far.astype(jnp.bfloat16).astype(jnp.float32)
            gap = corrected[b, :, cols].astype(jnp.float32) - far
            rhs[b * BLK : (b + 1) * BLK, cols] = (gap * weights[b]).astype(jnp.bfloat16)

    def consume(b, mine):
        dual[b] = (mine * weights[b]).astype(jnp.bfloat16)

    each_rows([], matrix, rhs, consume)
    pick_blocks(send, dual, slabs, range(DIRS))


def finish_kernel(read, mult, dual, *rest):
    arrived, (out, received, ready, sems) = rest[:DIRS], rest[DIRS:]
    stack_slabs(arrived, received, SECOND)
    copies = []
    for b in range(out.shape[0]):
        far = received[slot_read(read, b)]
        ready[b] = mult[b] + (dual[b].astype(jnp.float32) - far.astype(jnp.float32))
        copies.append(pltpu.make_async_copy(ready.at[b], out.at[b], sems.at[b]))
        copies[b].start()
    for copy in copies:
        copy.wait()


def pieces_of(lanes, cases):
    across = cases // BLK
    return [
        (i // 2, i % 2, i // across, slice(i % across * BLK, (i % across + 1) * BLK))
        for i in range(2 * (lanes // BLK))
    ]


def bring_kernel(matrix, after, held, sem):
    copy = pltpu.make_async_copy(matrix, held, sem)
    copy.start()
    copy.wait()


def share_kernel(wide, own_rows, mine, theirs, proj, *rest):
    near_basis, keep, give, held = rest[-4:]
    high, order = own_rows.shape
    subs, here = lax.axis_size("sub"), lax.axis_index("sub")
    chips = mine.shape[0]
    tall = (mine.shape[1] - NEAR) // 2
    sums = sum(names[p, NEAR:, :] for p in range(chips) for names in (mine, theirs))
    sums = sums.astype(jnp.int32) - 1

    def lanes_of(first):
        return jnp.concatenate([sums[first + r : first + r + 1] for r in range(tall)], axis=1)

    dofs, lanes = (lanes_of(0), lanes_of(tall)), subs * wide
    local = (lax.broadcasted_iota(jnp.int32, (high, lanes), 0) + here * high == dofs[0][:, :lanes])
    local = local.astype(jnp.float32).astype(jnp.bfloat16)
    source = own_rows[...].astype(jnp.bfloat16)
    for kind in range(2):
        pick = lax.broadcasted_iota(jnp.int32, (order, lanes), 0) == dofs[kind][:, :lanes]
        chosen = jnp.dot(
            source,
            pick.astype(jnp.float32).astype(jnp.bfloat16),
            preferred_element_type=jnp.float32,
        )
        held[kind] = lax.dot_general(
            chosen.astype(jnp.bfloat16),
            local,
            (((0,), (0,)), ((), ())),
            preferred_element_type=jnp.float32,
        )
    for e, target in enumerate((keep, give)):
        target[chips, : wide, :] = proj[...].astype(jnp.bfloat16)
        for p in range(chips):
            at = pl.ds(pl.multiple_of((here ^ (2 * p + e)) * wide, wide), wide)
            for q, kind, group, cols in pieces_of(lanes, target.shape[2]):
                target[p, group * wide : (group + 1) * wide, cols] = held[
                    kind, at, q * BLK : (q + 1) * BLK
                ].astype(jnp.bfloat16)
    for k in range(NEAR):
        sender = lax.rem(here - OFFSETS[k // CAP] + subs, subs) ^ here
        p, same = sender // 2, sender % 2 == 0
        near_basis[k : k + 1, :] = jnp.where(same, mine[p, k : k + 1], theirs[p, k : k + 1])


def merge_kernel(wide, chips, keep, got, *rest):
    for p, chunk in enumerate(rest[-chips:]):
        chunk[:wide, :] = keep[chips, :wide, :]
        chunk[wide : 2 * wide, :] = got[chips, :wide, :]
        chunk[2 * wide :, :] = keep[p] + got[p]


def on_device(
    load_cases,
    inv_schur,
    schur_blocks,
    coarse_basis,
    coarse_map,
    multiplicity,
    recv_code,
    send_blocks,
    coarse_inv,
):
    dofs = inv_schur.shape[2]
    cases = load_cases.shape[3]
    blocks = dofs // BLK
    subs = lax.axis_size("sub")
    chips = subs // 2
    wide = NEAR * -(-blocks // NEAR)
    lanes = subs * wide
    tall = 4 * -(-lanes // (4 * BLK))
    groups = -(-2 * (lanes // BLK) // (cases // BLK))
    solve_matrix = inv_schur[0, 0]
    dirichlet_matrix = schur_blocks[0, 0]
    load = load_cases[0, 0]
    read = recv_code[0, 0]
    send = send_blocks[0, 0]
    weights = 1.0 / multiplicity[0, 0].astype(jnp.float32)
    whole = f32(blocks, BLK, cases)
    halved = bf16(blocks, BLK, cases)
    slab = bf16(CAP, BLK, cases)
    block_columns = f32(blocks, BLK, BLK)
    received = pltpu.VMEM((DIRS * CAP, BLK, cases), jnp.bfloat16)
    narrow = pltpu.VMEM((blocks, BLK, cases), jnp.bfloat16)
    rhs = pltpu.VMEM((dofs, cases), jnp.bfloat16)
    steps = pltpu.SemaphoreType.DMA((dofs // ROWS,))
    resident = pltpu.VMEM((dofs, dofs), jnp.bfloat16)

    disp, proj, columns, told, *slabs, solve_matrix = pl.pallas_call(
        functools.partial(first_solve_kernel, wide),
        out_shape=[whole, f32(wide, cases), block_columns, f32(NEAR + 2 * tall, BLK)]
        + [slab] * EARLY[0]
        + [resident],
        in_specs=[HBM] * 5,
        out_specs=[VMEM] * (5 + EARLY[0]),
        scratch_shapes=[
            rhs,
            narrow,
            pltpu.SMEM((1, DIRS * CAP), jnp.int32),
            pltpu.SMEM((1, blocks), jnp.int32),
            pltpu.VMEM((1, dofs), jnp.float32),
            pltpu.VMEM((blocks, 1, BLK), jnp.float32),
            steps,
            pltpu.SemaphoreType.DMA((4,)),
        ],
        compiler_params=PARAMS,
    )(
        in_hbm(send_blocks[0]), in_hbm(coarse_map[0]), in_hbm(solve_matrix), in_hbm(load),
        in_hbm(coarse_basis[0]),
    )
    arrived = {way: exchanged(slabs[way], way) for way in ORDER if way < EARLY[0]}
    mine = jnp.stack(to_chips([told] * chips))
    theirs = swapped(mine, 1)
    outgoing = bf16(chips + 1, groups * wide, cases)
    near_basis, keep, give = pl.pallas_call(
        functools.partial(share_kernel, wide),
        out_shape=[f32(NEAR, BLK), outgoing, outgoing],
        in_specs=[VMEM] * 4 + [ANY] * 1,
        out_specs=[VMEM] * 3,
        scratch_shapes=[pltpu.VMEM((2, lanes, lanes), jnp.float32)],
        compiler_params=PARAMS,
    )(coarse_inv[0], mine, theirs, proj, arrived[4])
    chunks = pl.pallas_call(
        functools.partial(merge_kernel, wide, chips),
        out_shape=[bf16((2 + groups) * wide, cases)] * chips,
        in_specs=[VMEM] * 2 + [ANY] * 0,
        out_specs=[VMEM] * chips,
        compiler_params=PARAMS,
    )(keep, swapped(give, 1))
    parts = tables = to_chips(chunks)

    dirichlet_matrix = pl.pallas_call(
        bring_kernel,
        out_shape=resident,
        in_specs=[HBM, ANY],
        out_specs=VMEM,
        scratch_shapes=[pltpu.SemaphoreType.DMA],
        compiler_params=PARAMS,
    )(in_hbm(dirichlet_matrix), proj)

    for iteration in range(ITERS):
        early = EARLY[iteration]
        if iteration:
            arrived = {way: exchanged(slabs[way], way) for way in ORDER if way < early}
            proj = proj.astype(jnp.bfloat16)
            parts = to_chips([jnp.concatenate([proj, swapped(proj, 1)])] * chips)
        ties = [arrived[way] for way in (() if iteration == 0 else (4, 2, ))]
        corrected, near, *far = pl.pallas_call(
            functools.partial(coarse_kernel, wide, chips, early, len(ties)),
            out_shape=[halved, f32(NEAR, cases + BLK), f32(CAP, cases + BLK) if early > 4 else slab, slab],
            in_specs=[SMEM] + [VMEM] * 4 + [ANY] * len(ties) + [VMEM] * (2 * chips),
            out_specs=[VMEM] * 4,
            scratch_shapes=[
                pltpu.VMEM((lanes, cases), jnp.float32),
                pltpu.VMEM((blocks, 1, cases + BLK), jnp.float32),
            ],
            compiler_params=PARAMS,
        )(
            send, coarse_basis[0], near_basis, disp, columns, *ties, *parts, *tables,
        )
        arrived[5] = exchanged(far[1], 5)
        moved = exchanged(far[0], 4)
        if early == 4:
            arrived[4] = moved
        far_rows = [moved] * (early - 4)
        dual, *slabs = pl.pallas_call(
            functools.partial(dirichlet_kernel, early),
            out_shape=[halved] + [slab] * DIRS,
            in_specs=[SMEM] * 3 + [VMEM] * (early - 1 + DIRS),
            out_specs=[VMEM] * (1 + DIRS),
            scratch_shapes=[received, pltpu.VMEM((DIRS * CAP, 1, cases + BLK), jnp.float32), rhs],
            compiler_params=PARAMS,
        )(
            send, read, weights, dirichlet_matrix, corrected, near, *far_rows,
            *[arrived[way] for way in ORDER],
        )
        arrived = [exchanged(slabs[way], way) for way in SECOND]
        if iteration + 1 < ITERS:
            mult, disp, proj, *slabs = pl.pallas_call(
                next_solve_kernel,
                out_shape=[whole, whole, f32(wide, cases)] + [slab] * EARLY[iteration + 1],
                in_specs=[SMEM] * 2 + [VMEM] * (4 + DIRS),
                out_specs=[VMEM] * (3 + EARLY[iteration + 1]),
                scratch_shapes=[received, rhs, narrow],
                compiler_params=PARAMS,
            )(send, read, solve_matrix, load, columns, dual, *arrived)
    out = pl.pallas_call(
        finish_kernel,
        out_shape=whole,
        in_specs=[SMEM] + [VMEM] * (2 + DIRS),
        out_specs=HBM,
        scratch_shapes=[
            received,
            pltpu.VMEM((blocks, BLK, cases), jnp.float32),
            pltpu.SemaphoreType.DMA((blocks,)),
        ],
        compiler_params=PARAMS,
    )(read, mult, dual, *arrived)
    return out.reshape(1, 1, dofs, cases)


def solution(mesh):
    split = P("group", "sub")
    return jax.shard_map(
        on_device, mesh=mesh, in_specs=(split,) * 9, out_specs=split, check_vma=False
    )
```
